32 devices in a mesh: gx: 2 (over x), gy: 4 (over z), gz: 4 (over y, core).
Axes of the slice: x: 2, y: 2, z: 4, core: 2. Of those that a mesh axis runs over, the one named last changes fastest.
Arguments:
- u_start: float32 [8, 256, 512], P('gx', 'gy', 'gz'), may hold values from 0 to 1
- v_start: float32 [8, 256, 512], P('gx', 'gy', 'gz'), may hold values from 0 to 1
- w_start: float32 [8, 256, 512], P('gx', 'gy', 'gz'), may hold values from 0 to 1
- conduct: float32 [8, 256, 512], P('gx', 'gy', 'gz'), may hold values from 0.02 to 0.14
- direction: float32 [8, 256, 512], P('gx', 'gy', 'gz'), may hold values from -2.4 to 2.4
- obs_weight: float32 [8, 256, 512], P('gx', 'gy', 'gz'), may hold values from 0.25 to 12, as said below
- tissue: int32 [8, 256, 512], P('gx', 'gy', 'gz'), may hold values from 0 to 2
- stim_x: int32 [16], replicated, may hold values from 0 to 7
- stim_y: int32 [16], replicated, may hold values from 0 to 255
- stim_z: int32 [16], replicated, may hold values from 0 to 511
- stim_step: int32 [16], replicated, may hold values from 0 to 3
Outputs:
- hess_vec: float32 [8, 256, 512], P('gx', 'gy', 'gz')
- curvature: float32 [], replicated
The draws below stay inside these ranges and needn't reach their ends.
Inputs may be any that keep to these rules, and one draw needn't show every extreme that they name: 0 marks scar, 1 healthy tissue, 2 tissue with fibers along the first dimension. `obs_weight`: positive weights.
All inputs are finite; a program needn't handle non-finite values.
Results may differ from the reference program's by a relative error of at most 0.0003.
Values sent between devices are 32-bit elements; how exact they have to be, the bound alone decides.
A program may use at most 64 MiB of HBM per device.

```python
import math
from functools import partial
import jax
import jax.numpy as jnp
from jax import lax

STEPS = 4
NSTIM = 16
NX = 8
NY = 256
NZ = 512


def draw_obs_weight(key, part):
    lowest = math.log(0.25)
    ramp_x = 1.0 + 2.0 * jnp.arange(NX, dtype=jnp.float32) / max(NX - 1, 1)
    base = jnp.exp(jax.random.uniform(key, (NX, NY, NZ), jnp.float32, lowest, math.log(4.0)))
    return base * ramp_x[:, None, None]


def touch_ends(entries, rng, smallest, largest):
    extent = entries.shape
    place = [jax.random.randint(jax.random.fold_in(rng, axis), (), 0, extent[axis]) for axis in range(len(extent))]
    entries = entries.at[tuple(place)].set(smallest)
    longest = extent.index(max(extent))
    place[longest] = (place[longest] + 1) % extent[longest]
    return entries.at[tuple(place)].set(largest)


def level_of(key, extent, split, low, top_value):
    def one(axis_at, blocks):
        heights = jax.random.uniform(jax.random.fold_in(jax.random.fold_in(key, 6), axis_at), (blocks,), jnp.float32, low / len(split), top_value / len(split))
        return jnp.repeat(jnp.exp(heights), extent[axis_at] // blocks).reshape((-1,) + (1,) * (len(extent) - axis_at - 1))

    level = one(*split[0])
    for cut in split[1:]:
        level = level * one(*cut)
    return level


def noise(key, extent, scale, reach, shards=(), kind=jnp.bfloat16):
    factor_of = level_of(key, extent, shards, -0.22, 0.18) if shards else 1.0
    values = jax.random.normal(key, extent, jnp.float32) * scale * factor_of
    return jnp.minimum(jnp.maximum(values, -reach), reach).astype(kind)


def setup_inputs(seed: int = 0) -> dict:
    streams_of = jax.random.split(jax.random.key(seed), 12)
    return {
        "u_start": jnp.clip(1.0 * jax.random.uniform(streams_of[0], (NX, NY, NZ), jnp.float32) ** level_of(streams_of[0], (NX, NY, NZ), ((0, 2), (1, 4), (2, 4)), -0.2, 0.2), 0.0, 1.0),
        "v_start": jnp.clip(1.0 * jax.random.uniform(streams_of[1], (NX, NY, NZ), jnp.float32) ** level_of(streams_of[1], (NX, NY, NZ), ((0, 2), (1, 4), (2, 4)), -0.2, 0.2), 0.0, 1.0),
        "w_start": jnp.clip(1.0 * jax.random.uniform(streams_of[2], (NX, NY, NZ), jnp.float32) ** level_of(streams_of[2], (NX, NY, NZ), ((0, 2), (1, 4), (2, 4)), -0.2, 0.2), 0.0, 1.0),
        "conduct": jnp.clip(jnp.exp(math.log(0.14) - 1.9459102 * jax.random.uniform(streams_of[3], (NX, NY, NZ), jnp.float32) ** level_of(streams_of[3], (NX, NY, NZ), ((0, 2), (1, 4), (2, 4)), -0.2, 0.2)), 0.02, 0.14),
        "direction": noise(streams_of[4], (NX, NY, NZ), 0.3, 2.4, ((0, 2), (1, 4), (2, 4)), jnp.float32),
        "obs_weight": draw_obs_weight(jax.random.fold_in(streams_of[11], 71), 0),
        "tissue": touch_ends(jax.random.randint(streams_of[6], (NX, NY, NZ), 0, 3), jax.random.fold_in(streams_of[6], 1), 0, 2).astype(jnp.int32),
        "stim_x": touch_ends(jax.random.randint(streams_of[7], (NSTIM,), 0, NX), jax.random.fold_in(streams_of[7], 1), 0, NX - 1).astype(jnp.int32),
        "stim_y": touch_ends(jax.random.randint(streams_of[8], (NSTIM,), 0, NY), jax.random.fold_in(streams_of[8], 1), 0, NY - 1).astype(jnp.int32),
        "stim_z": touch_ends(jax.random.randint(streams_of[9], (NSTIM,), 0, NZ), jax.random.fold_in(streams_of[9], 1), 0, NZ - 1).astype(jnp.int32),
        "stim_step": touch_ends(jax.random.randint(streams_of[10], (NSTIM,), 0, STEPS), jax.random.fold_in(streams_of[10], 1), 0, STEPS - 1).astype(jnp.int32),
    }


time_step = 0.25
u_crit = 0.13
u_gate = 0.04
switch_width = 0.05
tau_fast = 0.4
tau_open = 12.5
tau_repol = 33.33
tau_slow = 15.0
k_slow = 10.0
u_slow = 0.85
tau_vplus = 3.33
tau_vminus_one = 19.6
tau_vminus_two = 1000.0
tau_wplus = 667.0
tau_wminus = 11.0
stim_amp = 2.0
tv_weight = 0.05
tv_smooth = 0.02

def switch(value):
    return 0.5 * (1.0 + jnp.tanh(value / switch_width))

def react(u_cell, v_gate, w_gate, stim_count):
    opened = switch(u_cell - u_crit)
    partly = switch(u_cell - u_gate)
    fast_in = -v_gate * opened * (1.0 - u_cell) * (u_cell - u_crit) / tau_fast
    slow_out = u_cell * (1.0 - opened) / tau_open + opened / tau_repol
    slow_in = -w_gate * (1.0 + jnp.tanh(k_slow * (u_cell - u_slow))) / (2.0 * tau_slow)
    u_next = u_cell + time_step * (stim_amp * stim_count - (fast_in + slow_out + slow_in))
    closed = 1.0 - opened
    v_rate = opened / tau_vplus + closed / (partly * tau_vminus_one + (1.0 - partly) * tau_vminus_two)
    w_rate = opened / tau_wplus + closed / tau_wminus
    v_next = closed + (v_gate - closed) * jnp.exp(-time_step * v_rate)
    w_next = closed + (w_gate - closed) * jnp.exp(-time_step * w_rate)
    return (u_next, v_next, w_next)

def kappas(tissue):
    scar = (tissue == 0).astype(jnp.float32)
    healthy = (tissue == 1).astype(jnp.float32)
    fiber = (tissue == 2).astype(jnp.float32)
    return (0.1 * scar + healthy + 1.5 * fiber, 0.1 * scar + healthy + 0.75 * fiber)

def shifted(padded, axis, offset):
    index = [slice(1, padded.shape[0] - 1), slice(1, padded.shape[1] - 1), slice(1, padded.shape[2] - 1)]
    index[axis] = slice(1 + offset, padded.shape[axis] - 1 + offset)
    return padded[tuple(index)]

def spread(along_c, across_c, live, values):
    centre = shifted(values, 0, 0)
    result = jnp.zeros(centre.shape, jnp.float32)
    for axis in range(3):
        coeff = along_c if axis == 0 else across_c
        own = shifted(coeff, axis, 0)
        for offset in (1, -1):
            face = 0.5 * (own + shifted(coeff, axis, offset)) * shifted(live, axis, offset)
            result = result + face * (shifted(values, axis, offset) - centre)
    return result

def sigma_term(along, across, live, u_pad, adj_pad):
    u_centre = shifted(u_pad, 0, 0)
    a_centre = shifted(adj_pad, 0, 0)
    parts = []
    for axis in range(3):
        part_sum = jnp.zeros(u_centre.shape, jnp.float32)
        for offset in (1, -1):
            part_sum = part_sum + 0.5 * (shifted(u_pad, axis, offset) - u_centre) * (a_centre - shifted(adj_pad, axis, offset)) * shifted(live, axis, offset)
        parts.append(part_sum)
    return along * parts[0] + across * (parts[1] + parts[2])

def forward_diff(padded, live, axis):
    lower = [slice(0, -1), slice(0, -1), slice(0, -1)]
    upper = [slice(0, -1), slice(0, -1), slice(0, -1)]
    upper[axis] = slice(1, None)
    return (padded[tuple(upper)] - padded[tuple(lower)]) * live[tuple(upper)] * live[tuple(lower)]

def tv_apply(sig_pad, dir_pad, live):
    diffs = [forward_diff(sig_pad, live, axis) for axis in range(3)]
    weight = 1.0 / jnp.sqrt(diffs[0] * diffs[0] + diffs[1] * diffs[1] + diffs[2] * diffs[2] + tv_smooth * tv_smooth)
    result = None
    for axis in range(3):
        flux = weight * forward_diff(dir_pad, live, axis)
        here = flux[1:, 1:, 1:]
        index = [slice(1, None), slice(1, None), slice(1, None)]
        index[axis] = slice(0, -1)
        term = flux[tuple(index)] - here
        result = term if result is None else result + term
    return result

def stimulus(step, xs_coord, ys_coord, zs_coord, stim_x, stim_y, stim_z, stim_step):
    active = (stim_step == step).astype(jnp.float32)
    near_x = (jnp.abs(xs_coord[None, :] - stim_x[:, None]) <= 1).astype(jnp.float32) * active[:, None]
    near_y = (jnp.abs(ys_coord[None, :] - stim_y[:, None]) <= 1).astype(jnp.float32)
    near_z = (jnp.abs(zs_coord[None, :] - stim_z[:, None]) <= 1).astype(jnp.float32)
    return jnp.einsum('si,sj,sk->ijk', near_x, near_y, near_z, precision=lax.Precision.HIGHEST)

def pad_one(array):
    return jnp.pad(array, 1)

def reference(u_start, v_start, w_start, conduct, direction, obs_weight, tissue, stim_x, stim_y, stim_z, stim_step):
    along, across = kappas(tissue)
    live = pad_one(jnp.ones(conduct.shape, jnp.float32))
    sig_pad = pad_one(conduct)
    dir_pad = pad_one(direction)
    along_pad = pad_one(along)
    across_pad = pad_one(across)
    c_along = along_pad * sig_pad
    c_across = across_pad * sig_pad
    d_along = along_pad * dir_pad
    d_across = across_pad * dir_pad
    xs_coord = jnp.arange(NX, dtype=jnp.int32)
    ys_coord = jnp.arange(NY, dtype=jnp.int32)
    zs_coord = jnp.arange(NZ, dtype=jnp.int32)
    u_cell, v_gate, w_gate = (u_start, v_start, w_start)
    du_cell = jnp.zeros(u_start.shape, jnp.float32)
    dv_gate = jnp.zeros(u_start.shape, jnp.float32)
    dw_gate = jnp.zeros(u_start.shape, jnp.float32)
    u_saved, v_saved, w_saved, du_saved = ([], [], [], [])
    for step in range(STEPS):
        u_pad = pad_one(u_cell)
        du_pad = pad_one(du_cell)
        u_saved.append(u_pad)
        v_saved.append(v_gate)
        w_saved.append(w_gate)
        stim_now = stimulus(step, xs_coord, ys_coord, zs_coord, stim_x, stim_y, stim_z, stim_step)
        primal, tangent = jax.jvp(partial(react, stim_count=stim_now), (u_cell, v_gate, w_gate), (du_cell, dv_gate, dw_gate))
        u_cell = primal[0] + spread(c_along, c_across, live, u_pad)
        du_cell = tangent[0] + spread(c_along, c_across, live, du_pad) + spread(d_along, d_across, live, u_pad)
        v_gate, w_gate = (primal[1], primal[2])
        dv_gate, dw_gate = (tangent[1], tangent[2])
        du_saved.append(du_cell)
    mean_weight = jnp.sum(obs_weight) / (NX * NY * NZ)
    scaled = obs_weight / mean_weight
    adj_u = scaled * du_saved[-1]
    adj_v = jnp.zeros(u_start.shape, jnp.float32)
    adj_w = jnp.zeros(u_start.shape, jnp.float32)
    gradient = jnp.zeros(u_start.shape, jnp.float32)
    zero_stim = jnp.zeros(u_start.shape, jnp.float32)
    for step in reversed(range(STEPS)):
        adj_pad = pad_one(adj_u)
        gradient = gradient + sigma_term(along, across, live, u_saved[step], adj_pad)
        if step > 0:
            _, pull = jax.vjp(partial(react, stim_count=zero_stim), shifted(u_saved[step], 0, 0), v_saved[step], w_saved[step])
            back_u, back_v, back_w = pull((adj_u, adj_v, adj_w))
            adj_u = back_u + spread(c_along, c_across, live, adj_pad) + scaled * du_saved[step - 1]
            adj_v, adj_w = (back_v, back_w)
    hess_vec = gradient + tv_weight * tv_apply(sig_pad, dir_pad, live)
    curvature = jnp.sum(direction * hess_vec)
    return (hess_vec, curvature)
```

```python
from functools import partial

import jax
import jax.numpy as jnp
from jax import lax
from jax.experimental import pallas as pl
from jax.experimental.pallas import tpu as pltpu
from jax.sharding import PartitionSpec as P

STEPS = 4
AXES = ("gx", "gy", "gz")

time_step = 0.25
u_crit = 0.13
u_gate = 0.04
switch_width = 0.05
tau_fast = 0.4
tau_open = 12.5
tau_repol = 33.33
tau_slow = 15.0
k_slow = 10.0
u_slow = 0.85
tau_vplus = 3.33
tau_vminus_one = 19.6
tau_vminus_two = 1000.0
tau_wplus = 667.0
tau_wminus = 11.0
stim_amp = 2.0
tv_weight = 0.05
tv_smooth = 0.02

ROWS = 16
TOP = 8
F32 = jnp.float32


def react(u, v, w, stim, primal, jac_u, jac_gates):
    out = {}
    opened = 0.5 * (1.0 + jnp.tanh((u - u_crit) * (1.0 / switch_width)))
    closed = 1.0 - opened
    slow = jnp.tanh(k_slow * (u - u_slow))
    hump = (1.0 - u) * (u - u_crit)
    uv = (time_step / tau_fast) * opened * hump
    uw = (time_step / (2.0 * tau_slow)) * (1.0 + slow)
    if primal:
        slow_out = u * closed * (1.0 / tau_open) + opened * (1.0 / tau_repol)
        out["u"] = u + (time_step * stim_amp) * stim + v * uv + w * uw - time_step * slow_out
    if jac_u or jac_gates:
        d_open = (2.0 / switch_width) * opened * closed
    if jac_u:
        d_hump = (1.0 + u_crit) - 2.0 * u
        d_fast = v * (1.0 / tau_fast) * (d_open * hump + opened * d_hump)
        d_out = closed * (1.0 / tau_open) + d_open * (1.0 / tau_repol - u * (1.0 / tau_open))
        d_in = w * (k_slow / (2.0 * tau_slow)) * (1.0 - slow * slow)
        out["uu"] = 1.0 + time_step * (d_fast - d_out + d_in)
        out["uv"] = uv
        out["uw"] = uw
    if primal or jac_gates:
        partly = 0.5 * (1.0 + jnp.tanh((u - u_gate) * (1.0 / switch_width)))
        slowness = 1.0 / (partly * tau_vminus_one + (1.0 - partly) * tau_vminus_two)
        keep_v = jnp.exp(-time_step * (opened * (1.0 / tau_vplus) + closed * slowness))
        keep_w = jnp.exp(-time_step * (opened * (1.0 / tau_wplus) + closed * (1.0 / tau_wminus)))
        far_v = (v - closed) * keep_v
        far_w = (w - closed) * keep_w
        out["v"] = closed + far_v
        out["w"] = closed + far_w
        out["vv"] = keep_v
        out["ww"] = keep_w
    if jac_gates:
        d_partly = (2.0 / switch_width) * partly * (1.0 - partly)
        d_rate_v = d_open * (1.0 / tau_vplus - slowness) + closed * d_partly * (
            (tau_vminus_two - tau_vminus_one) * slowness * slowness
        )
        d_rate_w = d_open * (1.0 / tau_wplus - 1.0 / tau_wminus)
        out["vu"] = d_open * (keep_v - 1.0) - time_step * far_v * d_rate_v
        out["wu"] = d_open * (keep_w - 1.0) - time_step * far_w * d_rate_w
    return out


def kernel(
    sizes,
    u_in,
    v_in,
    w_in,
    c_in,
    d_in,
    obs_in,
    tissue_in,
    sx_in,
    sy_in,
    sz_in,
    ss_in,
    hess_out,
    curv_out,
    pot,
    adj,
    kal,
    kac,
    cd,
    face,
    gates,
    dgates,
    bgates,
    jac,
    local,
    stim,
    zdiff,
    grad,
    qx,
    qy,
    qz,
    sums,
    zsend,
    zrecv,
    ysend,
    yrecv,
    red_own,
    red_x,
    red_y,
    red_z,
    send_sem,
    recv_sem,
    rsend_sem,
    rrecv_sem,
):
    X, Y, Z = u_in.shape
    chunks = Y // ROWS
    place = [lax.axis_index(a) for a in AXES]
    has_lo = [p > 0 for p in place]
    has_hi = [p < n - 1 for p, n in zip(place, sizes)]
    lo_flag = [h.astype(F32) for h in has_lo]
    hi_flag = [h.astype(F32) for h in has_hi]

    barrier = pltpu.get_barrier_semaphore()
    for a, n in enumerate(sizes):
        for k in range(1, n):
            pl.semaphore_signal(
                barrier,
                inc=1,
                device_id={AXES[a]: lax.rem(place[a] + k, n)},
                device_id_type=pl.DeviceIdType.MESH,
            )

    lane = lax.broadcasted_iota(jnp.int32, (ROWS, Z), 1)
    row = lax.broadcasted_iota(jnp.int32, (ROWS, Z), 0)
    blk = pl.ds(TOP, Y)

    pending = []
    counter = [0]

    def send(axis, up, src, dst):
        slot = counter[0]
        counter[0] += 1
        step = 1 if up else -1
        n = sizes[axis]
        target = lax.rem(place[axis] + step + n, n)
        copy = pltpu.make_async_remote_copy(
            src_ref=src,
            dst_ref=dst,
            send_sem=send_sem.at[slot],
            recv_sem=recv_sem.at[slot],
            device_id={AXES[axis]: target},
            device_id_type=pl.DeviceIdType.MESH,
        )
        to = has_hi[axis] if up else has_lo[axis]
        fro = has_lo[axis] if up else has_hi[axis]

        @pl.when(to)
        def _():
            copy.start()

        def wait_send():
            @pl.when(to)
            def _():
                copy.wait_send()

        def wait_recv():
            @pl.when(fro)
            def _():
                copy.wait_recv()

        pending.append(wait_send)
        return wait_recv

    def over(body, group=None):
        xs = tuple(range(X)) if group is None else group

        def one(j, carry):
            y0 = pl.multiple_of(j * ROWS, ROWS)
            for x in xs:
                body(x, y0)
            return carry

        lax.fori_loop(0, chunks, one, 0)

    def pack_z(r, which, x, y0, value, first, up=True, down=True):
        k = which * X + x
        rows = pl.ds(y0, ROWS)
        for side, wanted, shift in ((0, up, (k + 1) % Z), (1, down, k)):
            if wanted:
                moved = pltpu.roll(value, shift, 1) if shift else value
                if not first:
                    moved = jnp.where(lane == k, moved, zsend[r, side, rows])
                zsend[r, side, rows] = moved

    def from_z(r, which, x, y0, value, lo=True, hi=True):
        k = which * X + x
        rows = pl.ds(y0, ROWS)
        zm = zp = None
        if lo:
            edge = zrecv[r, 0, rows]
            edge = pltpu.roll(edge, Z - k, 1) if k else edge
            zm = jnp.where(lane == 0, edge, pltpu.roll(value, 1, 1))
        if hi:
            zp = jnp.where(
                lane == Z - 1,
                pltpu.roll(zrecv[r, 1, rows], Z - 1 - k, 1),
                pltpu.roll(value, Z - 1, 1),
            )
        return zm, zp

    def send_y(r, refs, ups, downs):
        for f, ref in enumerate(refs):
            for x in range(X):
                k = f * X + x
                if f < ups:
                    ysend[r, 0, k : k + 1] = ref(x)[TOP + Y - 1 : TOP + Y]
                if f < downs:
                    ysend[r, 1, k : k + 1] = ref(x)[TOP : TOP + 1]
        waits = []
        for side, count, up in ((0, ups, True), (1, downs, False)):
            if count:
                waits.append(send(1, up, ysend.at[r, side], yrecv.at[r, side]))
        return waits

    def unpack_y(r, refs, ups, downs):
        for f, ref in enumerate(refs):
            for x in range(X):
                k = f * X + x
                if f < ups:
                    ref(x)[TOP - 1 : TOP] = yrecv[r, 0, k : k + 1]
                if f < downs:
                    ref(x)[TOP + Y : TOP + Y + 1] = yrecv[r, 1, k : k + 1]

    def send_z(r, up=True, down=True):
        waits = []
        if up:
            waits.append(send(2, True, zsend.at[r, 0], zrecv.at[r, 0]))
        if down:
            waits.append(send(2, False, zsend.at[r, 1], zrecv.at[r, 1]))
        return waits

    outer = (0,) if X == 1 else (0, X - 1)
    inner = tuple(range(1, X - 1))

    def begin(x, y0):
        rows, prow = pl.ds(y0, ROWS), pl.ds(y0 + TOP, ROWS)
        tissue = tissue_in[x, rows]
        u, c, d = u_in[x, rows], c_in[x, rows], d_in[x, rows]
        along = jnp.where(tissue == 0, 0.1, jnp.where(tissue == 1, 1.0, 1.5))
        across = jnp.where(tissue == 0, 0.1, jnp.where(tissue == 1, 1.0, 0.75))
        cx, dx = across * c, across * d
        pot[0, 0, x + 1, prow] = u
        kal[0, x + 1, rows] = along * c
        kal[1, x + 1, rows] = along * d
        kac[0, x, prow] = cx
        kac[1, x, prow] = dx
        cd[0, x + 1, prow] = c
        cd[1, x + 1, prow] = d
        for f, value in enumerate((u, cx, dx, c, d)):
            pack_z(0, f, x, y0, value, x == 0 and f == 0, up=f < 3)

    over(begin, outer)
    pl.semaphore_wait(barrier, sum(n - 1 for n in sizes))
    waits = [
        send(0, True, pot.at[0, 0, X, blk], pot.at[0, 0, 0, blk]),
        send(0, False, pot.at[0, 0, 1, blk], pot.at[0, 0, X + 1, blk]),
        send(0, True, kal.at[:, X], kal.at[:, 0]),
        send(0, False, kal.at[:, 1], kal.at[:, X + 1]),
    ]
    over(begin, inner)
    refs0 = (
        lambda x: pot.at[0, 0, x + 1],
        lambda x: kac.at[0, x],
        lambda x: kac.at[1, x],
        lambda x: cd.at[0, x + 1],
        lambda x: cd.at[1, x + 1],
    )
    waits += send_y(0, refs0, 3, 5)
    waits += send_z(0)
    late = [send(0, False, cd.at[:, 1, blk], cd.at[:, X + 1, blk])]

    def clear(axis, lo, refs):
        @pl.when(jnp.logical_not(has_lo[axis] if lo else has_hi[axis]))
        def _():
            for ref in refs:
                ref[...] = jnp.zeros(ref.shape, F32)

    for lo, p in ((True, 0), (False, X + 1)):
        clear(0, lo, [pot.at[:, :, p], adj.at[:, p], kal.at[:, p]])
    clear(0, False, [cd.at[:, X + 1]])
    clear(0, True, [qx.at[0]])
    for lo, side in ((True, 0), (False, 1)):
        clear(1, lo, [yrecv.at[:, side]])
        clear(2, lo, [zrecv.at[:, side]])

    sx, sy, sz, ss = sx_in[...], sy_in[...], sz_in[...], ss_in[...]
    sites = sx.shape[1]
    ys = place[1] * Y + lax.broadcasted_iota(jnp.int32, (Y, sites), 0)
    zs = place[2] * Z + lax.broadcasted_iota(jnp.int32, (Z, sites), 0)
    near_y = (jnp.abs(ys - sy) <= 1).astype(F32)
    near_z = (jnp.abs(zs - sz) <= 1).astype(F32)
    for t in range(STEPS - 1):
        for x in range(X):
            near_x = jnp.where(ss == t, (jnp.abs(place[0] * X + x - sx) <= 1).astype(F32), 0.0)
            stim[t, x] = lax.dot_general(
                near_y * near_x, near_z, (((1,), (1,)), ((), ())), preferred_element_type=F32
            )

    def local_forward(t):
        last = t == STEPS - 1

        def body(x, y0):
            rows, prow = pl.ds(y0, ROWS), pl.ds(y0 + TOP, ROWS)
            u = pot[t, 0, x + 1, prow]
            if t == 0:
                v, w = v_in[x, rows], w_in[x, rows]
            else:
                v, w = gates[t, 0, x, rows], gates[t, 1, x, rows]
            n = None if last else stim[t, x, rows]
            e = react(u, v, w, n, not last, t > 0, 0 < t < STEPS - 1)
            if not last:
                local[0, x, rows] = e["u"]
                gates[t + 1, 0, x, rows] = e["v"]
                gates[t + 1, 1, x, rows] = e["w"]
            if t > 0:
                du = pot[t, 1, x + 1, prow]
                dlocal = e["uu"] * du
                jac[t, 0, x, rows] = e["uu"]
                if t > 1:
                    dv, dw = dgates[t, 0, x, rows], dgates[t, 1, x, rows]
                    dlocal = dlocal + e["uv"] * dv + e["uw"] * dw
                    jac[t, 1, x, rows] = e["uv"]
                    jac[t, 2, x, rows] = e["uw"]
                local[1, x, rows] = dlocal
                if not last:
                    jac[t, 3, x, rows] = e["vu"]
                    jac[t, 4, x, rows] = e["wu"]
                    new_dv, new_dw = e["vu"] * du, e["wu"] * du
                    if t > 1:
                        jac[t, 5, x, rows] = e["vv"]
                        jac[t, 6, x, rows] = e["ww"]
                        new_dv = new_dv + e["vv"] * dv
                        new_dw = new_dw + e["ww"] * dw
                    dgates[t + 1, 0, x, rows] = new_dv
                    dgates[t + 1, 1, x, rows] = new_dw

        over(body)

    def neighbours(ref, r, which, x, y0):
        value = ref[x + 1, pl.ds(y0 + TOP, ROWS)]
        zm, zp = from_z(r, which, x, y0, value)
        return value, (
            ref[x, pl.ds(y0 + TOP, ROWS)],
            ref[x + 2, pl.ds(y0 + TOP, ROWS)],
            ref[x + 1, pl.ds(y0 + TOP - 1, ROWS)],
            ref[x + 1, pl.ds(y0 + TOP + 1, ROWS)],
            zm,
            zp,
        )

    def face_weights(x, y0):
        rows, prow = pl.ds(y0, ROWS), pl.ds(y0 + TOP, ROWS)
        live = (
            lo_flag[0] if x == 0 else None,
            hi_flag[0] if x == X - 1 else None,
            jnp.where(y0 + row == 0, lo_flag[1], 1.0),
            jnp.where(y0 + row == Y - 1, hi_flag[1], 1.0),
            jnp.where(lane == 0, lo_flag[2], 1.0),
            jnp.where(lane == Z - 1, hi_flag[2], 1.0),
        )
        weights = []
        for f in range(2):
            own = kal[f, x + 1, rows]
            mine = kac[f, x, prow]
            zm, zp = from_z(0, 1 + f, x, y0, mine)
            raw = (
                own + kal[f, x, rows],
                own + kal[f, x + 2, rows],
                mine + kac[f, x, pl.ds(y0 + TOP - 1, ROWS)],
                mine + kac[f, x, pl.ds(y0 + TOP + 1, ROWS)],
                mine + zm,
                mine + zp,
            )
            out = []
            for i in range(6):
                weight = 0.5 * raw[i]
                if live[i] is not None:
                    weight = weight * live[i]
                face[f, i, x, rows] = weight
                out.append(weight)
            weights.append(out)
        return weights

    def dot6(weights, diffs):
        return (weights[0] * diffs[0] + weights[1] * diffs[1]) + (
            (weights[2] * diffs[2] + weights[3] * diffs[3])
            + (weights[4] * diffs[4] + weights[5] * diffs[5])
        )

    def stencil_forward(t):
        last = t == STEPS - 1

        def body(x, y0):
            rows, prow = pl.ds(y0, ROWS), pl.ds(y0 + TOP, ROWS)
            u, around = neighbours(pot.at[t, 0], t, 0, x, y0)
            diffs = [value - u for value in around]
            zdiff[t, 0, x, rows] = diffs[4]
            zdiff[t, 1, x, rows] = diffs[5]
            if t == 0:
                wc, wd = face_weights(x, y0)
            else:
                wc = [face[0, i, x, rows] for i in range(6)]
                wd = [face[1, i, x, rows] for i in range(6)]
            new_du = dot6(wd, diffs)
            if t > 0:
                du, around = neighbours(pot.at[t, 1], t, 1, x, y0)
                new_du = new_du + local[1, x, rows] + dot6(wc, [value - du for value in around])
            obs = obs_in[x, rows]
            weighted = obs * new_du
            if t == 0:
                sums[0, :, :] += obs
            sums[1, :, :] += weighted * new_du
            if last:
                adj[t, x + 1, prow] = weighted
                pack_z(t + 1, 0, x, y0, weighted, x == 0)
            else:
                new_u = local[0, x, rows] + dot6(wc, diffs)
                pot[t + 1, 0, x + 1, prow] = new_u
                pot[t + 1, 1, x + 1, prow] = new_du
                pack_z(t + 1, 0, x, y0, new_u, x == 0)
                pack_z(t + 1, 1, x, y0, new_du, False)

        return body

    def send_x_adj(t):
        return [
            send(0, True, adj.at[t, X, blk], adj.at[t, 0, blk]),
            send(0, False, adj.at[t, 1, blk], adj.at[t, X + 1, blk]),
        ]

    def send_x_pot(t):
        return [
            send(0, True, pot.at[t, :, X, blk], pot.at[t, :, 0, blk]),
            send(0, False, pot.at[t, :, 1, blk], pot.at[t, :, X + 1, blk]),
        ]

    def prior_flux():
        def body(x, y0):
            rows, prow = pl.ds(y0, ROWS), pl.ds(y0 + TOP, ROWS)
            live_y = jnp.where(y0 + row == Y - 1, hi_flag[1], 1.0)
            live_z = jnp.where(lane == Z - 1, hi_flag[2], 1.0)
            steps = []
            for f in range(2):
                own = cd[f, x + 1, prow]
                dx = cd[f, x + 2, prow] - own
                if x == X - 1:
                    dx = dx * hi_flag[0]
                dy = (cd[f, x + 1, pl.ds(y0 + TOP + 1, ROWS)] - own) * live_y
                dz = (from_z(0, 3 + f, x, y0, own, lo=False)[1] - own) * live_z
                steps.append((dx, dy, dz))
            (a, b, c), (p, q, r) = steps
            m = lax.rsqrt(a * a + b * b + c * c + tv_smooth * tv_smooth)
            sums[2, :, :] += m * (p * p + q * q + r * r)
            qx[x + 1, rows] = m * p
            qy[x, prow] = m * q
            flux = m * r
            qz[x, rows] = flux
            pack_z(2 * STEPS, 0, x, y0, flux, x == 0, down=False)

        over(body)

    sums[...] = jnp.zeros(sums.shape, F32)
    refs_u = lambda t: (lambda x: pot.at[t, 0, x + 1], lambda x: pot.at[t, 1, x + 1])
    refs_a = lambda t: (lambda x: adj.at[t, x + 1],)
    refs_q = (lambda x: qy.at[x],)
    qr = 2 * STEPS
    for t in range(STEPS):
        local_forward(t)
        if t == 1:
            for wait in late:
                wait()
            prior_flux()
        for wait in waits:
            wait()
        if t == 0:
            unpack_y(0, refs0, 3, 5)
        else:
            unpack_y(t, refs_u(t), 2, 2)
        body = stencil_forward(t)
        over(body, outer)
        if t == STEPS - 1:
            waits = send_x_adj(t)
            over(body, inner)
            waits += send_y(t + 1, refs_a(t), 1, 1)
            waits += send_z(t + 1)
        else:
            waits = send_x_pot(t + 1)
            over(body, inner)
            waits += send_y(t + 1, refs_u(t + 1), 2, 2)
            waits += send_z(t + 1)
        if t == 1:
            late = [send(0, True, qx.at[X], qx.at[0])]
            late += send_y(qr, refs_q, 1, 0)
            late += send_z(qr, down=False)

    red_bufs = (red_x, red_y, red_z)
    red_base = (0, sizes[0] - 1, sizes[0] + sizes[1] - 2)

    def reduce_start(axis, value):
        n, buf, me = sizes[axis], red_bufs[axis], place[axis]
        red_own[axis] = value
        buf[pl.ds(me, 1)] = value[None]
        waits = []
        for k in range(1, n):
            slot = red_base[axis] + k - 1
            copy = pltpu.make_async_remote_copy(
                src_ref=red_own.at[axis],
                dst_ref=buf.at[me],
                send_sem=rsend_sem.at[slot],
                recv_sem=rrecv_sem.at[slot],
                device_id={AXES[axis]: lax.rem(me + k, n)},
                device_id_type=pl.DeviceIdType.MESH,
            )
            copy.start()
            pending.append(copy.wait_send)
            arrival = pltpu.make_async_remote_copy(
                src_ref=red_own.at[axis],
                dst_ref=buf.at[lax.rem(me + n - k, n)],
                send_sem=rsend_sem.at[slot],
                recv_sem=rrecv_sem.at[slot],
                device_id={AXES[axis]: lax.rem(me + k, n)},
                device_id_type=pl.DeviceIdType.MESH,
            )
            waits.append(arrival.wait_recv)
        return waits

    def reduce_end(axis, waits):
        for wait in waits:
            wait()
        total = red_bufs[axis][0]
        for i in range(1, sizes[axis]):
            total = total + red_bufs[axis][i]
        return total

    part_row = lax.broadcasted_iota(jnp.int32, (8, Z), 0)
    parts = jnp.zeros((8, Z), F32)
    for i in range(3):
        parts = parts + jnp.where(part_row == i, jnp.sum(sums[i], axis=0, keepdims=True), 0.0)
    reduced = reduce_start(2, parts)

    def local_backward(t):
        def body(x, y0):
            rows, prow = pl.ds(y0, ROWS), pl.ds(y0 + TOP, ROWS)
            a = adj[t, x + 1, prow]
            new = jac[t, 0, x, rows] * a
            if t < STEPS - 1:
                b, c = bgates[t + 1, 0, x, rows], bgates[t + 1, 1, x, rows]
                new = new + jac[t, 3, x, rows] * b + jac[t, 4, x, rows] * c
            local[0, x, rows] = new + obs_in[x, rows] * pot[t, 1, x + 1, prow]
            if t > 1:
                new_b = jac[t, 1, x, rows] * a
                new_c = jac[t, 2, x, rows] * a
                if t < STEPS - 1:
                    new_b = new_b + jac[t, 5, x, rows] * b
                    new_c = new_c + jac[t, 6, x, rows] * c
                bgates[t, 0, x, rows] = new_b
                bgates[t, 1, x, rows] = new_c

        over(body)

    def stencil_backward(t):
        def body(x, y0):
            rows, prow = pl.ds(y0, ROWS), pl.ds(y0 + TOP, ROWS)
            a, around = neighbours(adj.at[t], STEPS + (STEPS - 1 - t), 0, x, y0)
            diffs = [value - a for value in around]
            if t > 0:
                wc = [face[0, i, x, rows] for i in range(6)]
                new = local[0, x, rows] + dot6(wc, diffs)
                adj[t - 1, x + 1, prow] = new
                pack_z(STEPS + (STEPS - t), 0, x, y0, new, x == 0)
            ref = pot.at[t, 0]
            u = ref[x + 1, prow]
            px = (ref[x, prow] - u) * diffs[0] * (lo_flag[0] if x == 0 else 1.0)
            px = px + (ref[x + 2, prow] - u) * diffs[1] * (hi_flag[0] if x == X - 1 else 1.0)
            live = [
                jnp.where(y0 + row == 0, lo_flag[1], 1.0),
                jnp.where(y0 + row == Y - 1, hi_flag[1], 1.0),
                jnp.where(lane == 0, lo_flag[2], 1.0),
                jnp.where(lane == Z - 1, hi_flag[2], 1.0),
            ]
            u_diffs = [
                ref[x + 1, pl.ds(y0 + TOP - 1, ROWS)] - u,
                ref[x + 1, pl.ds(y0 + TOP + 1, ROWS)] - u,
                zdiff[t, 0, x, rows],
                zdiff[t, 1, x, rows],
            ]
            pyz = sum(u_diffs[i] * diffs[2 + i] * live[i] for i in range(4))
            tissue = tissue_in[x, rows]
            along = jnp.where(tissue == 0, -0.05, jnp.where(tissue == 1, -0.5, -0.75))
            across = jnp.where(tissue == 0, -0.05, jnp.where(tissue == 1, -0.5, -0.375))
            term = along * px + across * pyz
            if t < STEPS - 1:
                term = term + grad[x, rows]
            grad[x, rows] = term

        return body

    for t in reversed(range(STEPS)):
        r = STEPS + (STEPS - 1 - t)
        if t > 0:
            local_backward(t)
        for wait in waits:
            wait()
        unpack_y(r, refs_a(t), 1, 1)
        body = stencil_backward(t)
        over(body, outer)
        if t > 0:
            waits = send_x_adj(t - 1)
            over(body, inner)
            waits += send_y(r + 1, refs_a(t - 1), 1, 1)
            waits += send_z(r + 1)
            if t == STEPS - 1:
                reduced = reduce_start(1, reduce_end(2, reduced))
            if t == STEPS - 2:
                reduced = reduce_start(0, reduce_end(1, reduced))
        else:
            over(body, inner)
    total = reduce_end(0, reduced)

    for wait in late:
        wait()
    unpack_y(qr, refs_q, 1, 0)
    voxels = float(X * sizes[0]) * float(Y * sizes[1]) * float(Z * sizes[2])
    factor = voxels / jnp.sum(total[0:1], axis=1, keepdims=True)
    misfit = jnp.sum(total[1:2], axis=1, keepdims=True)
    smooth = jnp.sum(total[2:3], axis=1, keepdims=True)
    curv_out[...] = factor * misfit + tv_weight * smooth

    def finish(x, y0):
        rows, prow = pl.ds(y0, ROWS), pl.ds(y0 + TOP, ROWS)
        here = qz[x, rows]
        prior = (
            (qx[x, rows] - qx[x + 1, rows])
            + (qy[x, pl.ds(y0 + TOP - 1, ROWS)] - qy[x, prow])
            + (from_z(qr, 0, x, y0, here, hi=False)[0] - here)
        )
        hess_out[x, rows] = grad[x, rows] * factor + tv_weight * prior

    over(finish)
    for wait in pending:
        wait()


def shards(sizes, *args):
    X, Y, Z = args[0].shape
    dense = lambda *lead: pltpu.VMEM((*lead, Y, Z), F32)
    tall = lambda *lead: pltpu.VMEM((*lead, Y + 2 * TOP, Z), F32)
    lines = sum(n - 1 for n in sizes)
    rounds = 2 * STEPS + 1
    face_rows = -(-5 * X // 8) * 8
    copies = 9 + 6 * (STEPS - 1) + 6 * STEPS + 3
    vmem = pl.BlockSpec(memory_space=pltpu.VMEM)
    stims = [a.reshape(1, a.shape[0]) for a in args[7:]]
    hess, curv = pl.pallas_call(
        partial(kernel, sizes),
        out_shape=(
            jax.ShapeDtypeStruct((X, Y, Z), F32),
            jax.ShapeDtypeStruct((1, 1), F32),
        ),
        in_specs=[vmem] * 11,
        out_specs=(vmem, vmem),
        scratch_shapes=[
            tall(STEPS, 2, X + 2),
            tall(STEPS, X + 2),
            dense(2, X + 2),
            tall(2, X),
            tall(2, X + 2),
            dense(2, 6, X),
            dense(STEPS, 2, X),
            dense(STEPS, 2, X),
            dense(STEPS, 2, X),
            dense(STEPS, 7, X),
            dense(2, X),
            dense(STEPS - 1, X),
            dense(STEPS, 2, X),
            dense(X),
            dense(X + 1),
            tall(X),
            dense(X),
            pltpu.VMEM((3, ROWS, Z), F32),
            dense(rounds, 2),
            dense(rounds, 2),
            pltpu.VMEM((rounds, 2, face_rows, Z), F32),
            pltpu.VMEM((rounds, 2, face_rows, Z), F32),
            pltpu.VMEM((3, 8, Z), F32),
            pltpu.VMEM((sizes[0], 8, Z), F32),
            pltpu.VMEM((sizes[1], 8, Z), F32),
            pltpu.VMEM((sizes[2], 8, Z), F32),
            pltpu.SemaphoreType.DMA((copies,)),
            pltpu.SemaphoreType.DMA((copies,)),
            pltpu.SemaphoreType.DMA((lines,)),
            pltpu.SemaphoreType.DMA((lines,)),
        ],
        compiler_params=pltpu.CompilerParams(
            collective_id=0, has_side_effects=True, vmem_limit_bytes=40 * 1024 * 1024
        ),
    )(*args[:7], *stims)
    return hess, curv.reshape(())


def solution(mesh):
    sizes = tuple(mesh.shape[a] for a in AXES)
    split = P(*AXES)
    return jax.shard_map(
        partial(shards, sizes),
        mesh=mesh,
        in_specs=(split,) * 7 + (P(),) * 4,
        out_specs=(split, P()),
        check_vma=False,
    )
```

```python
from functools import partial

import jax
import jax.numpy as jnp
from jax import lax
from jax.experimental import pallas as pl
from jax.experimental.pallas import tpu as pltpu
from jax.sharding import PartitionSpec as P

STEPS = 4
AXES = ("gx", "gy", "gz")

time_step = 0.25
u_crit = 0.13
u_gate = 0.04
switch_width = 0.05
tau_fast = 0.4
tau_open = 12.5
tau_repol = 33.33
tau_slow = 15.0
k_slow = 10.0
u_slow = 0.85
tau_vplus = 3.33
tau_vminus_one = 19.6
tau_vminus_two = 1000.0
tau_wplus = 667.0
tau_wminus = 11.0
stim_amp = 2.0
tv_weight = 0.05
tv_smooth = 0.02

ROWS = 64
TOP = 8
F32 = jnp.float32


def react(u, v, w, stim, primal, jac_u, jac_gates):
    out = {}
    opened = 0.5 * (1.0 + jnp.tanh((u - u_crit) * (1.0 / switch_width)))
    closed = 1.0 - opened
    slow = jnp.tanh(k_slow * (u - u_slow))
    hump = (1.0 - u) * (u - u_crit)
    uv = (time_step / tau_fast) * opened * hump
    uw = (time_step / (2.0 * tau_slow)) * (1.0 + slow)
    if primal:
        slow_out = u * closed * (1.0 / tau_open) + opened * (1.0 / tau_repol)
        out["u"] = u + (time_step * stim_amp) * stim + v * uv + w * uw - time_step * slow_out
    if jac_u or jac_gates:
        d_open = (2.0 / switch_width) * opened * closed
    if jac_u:
        d_hump = (1.0 + u_crit) - 2.0 * u
        d_fast = v * (1.0 / tau_fast) * (d_open * hump + opened * d_hump)
        d_out = closed * (1.0 / tau_open) + d_open * (1.0 / tau_repol - u * (1.0 / tau_open))
        d_in = w * (k_slow / (2.0 * tau_slow)) * (1.0 - slow * slow)
        out["uu"] = 1.0 + time_step * (d_fast - d_out + d_in)
        out["uv"] = uv
        out["uw"] = uw
    if primal or jac_gates:
        partly = 0.5 * (1.0 + jnp.tanh((u - u_gate) * (1.0 / switch_width)))
        slowness = 1.0 / (partly * tau_vminus_one + (1.0 - partly) * tau_vminus_two)
        keep_v = jnp.exp(-time_step * (opened * (1.0 / tau_vplus) + closed * slowness))
        keep_w = jnp.exp(-time_step * (opened * (1.0 / tau_wplus) + closed * (1.0 / tau_wminus)))
        far_v = (v - closed) * keep_v
        far_w = (w - closed) * keep_w
        out["v"] = closed + far_v
        out["w"] = closed + far_w
        out["vv"] = keep_v
        out["ww"] = keep_w
    if jac_gates:
        d_partly = (2.0 / switch_width) * partly * (1.0 - partly)
        d_rate_v = d_open * (1.0 / tau_vplus - slowness) + closed * d_partly * (
            (tau_vminus_two - tau_vminus_one) * slowness * slowness
        )
        d_rate_w = d_open * (1.0 / tau_wplus - 1.0 / tau_wminus)
        out["vu"] = d_open * (keep_v - 1.0) - time_step * far_v * d_rate_v
        out["wu"] = d_open * (keep_w - 1.0) - time_step * far_w * d_rate_w
    return out


def kernel(
    sizes,
    u_hbm,
    v_hbm,
    w_hbm,
    c_hbm,
    d_hbm,
    obs_hbm,
    tissue_hbm,
    sx_hbm,
    sy_hbm,
    sz_hbm,
    ss_hbm,
    hess_out,
    curv_out,
    u_in,
    v_in,
    w_in,
    c_in,
    d_in,
    obs_in,
    tissue_in,
    sx_in,
    sy_in,
    sz_in,
    ss_in,
    pot,
    adj,
    kal,
    kac,
    cd,
    face,
    gates,
    dgates,
    bgates,
    jac,
    local,
    stim,
    zdiff,
    grad,
    qx,
    qy,
    qz,
    sums,
    zsend,
    zrecv,
    ysend,
    yrecv,
    red_own,
    red_x,
    red_y,
    red_z,
    send_sem,
    recv_sem,
    rsend_sem,
    rrecv_sem,
    load_sem,
):
    pairs = (
        (tissue_hbm, tissue_in),
        (u_hbm, u_in),
        (c_hbm, c_in),
        (d_hbm, d_in),
        (sx_hbm, sx_in),
        (sy_hbm, sy_in),
        (sz_hbm, sz_in),
        (ss_hbm, ss_in),
        (v_hbm, v_in),
        (w_hbm, w_in),
        (obs_hbm, obs_in),
    )
    loads = [pltpu.make_async_copy(a, b, load_sem.at[i]) for i, (a, b) in enumerate(pairs)]
    for load in loads:
        load.start()
    X, Y, Z = u_in.shape
    chunks = Y // ROWS
    place = [lax.axis_index(a) for a in AXES]
    has_lo = [p > 0 for p in place]
    has_hi = [p < n - 1 for p, n in zip(place, sizes)]
    lo_flag = [h.astype(F32) for h in has_lo]
    hi_flag = [h.astype(F32) for h in has_hi]

    barrier = pltpu.get_barrier_semaphore()
    for a, n in enumerate(sizes):
        for k in range(1, n):
            pl.semaphore_signal(
                barrier,
                inc=1,
                device_id={AXES[a]: lax.rem(place[a] + k, n)},
                device_id_type=pl.DeviceIdType.MESH,
            )

    lane = lax.broadcasted_iota(jnp.int32, (ROWS, Z), 1)
    row = lax.broadcasted_iota(jnp.int32, (ROWS, Z), 0)
    blk = pl.ds(TOP, Y)

    pending = []
    counter = [0]

    def send(axis, up, src, dst):
        slot = counter[0]
        counter[0] += 1
        step = 1 if up else -1
        n = sizes[axis]
        target = lax.rem(place[axis] + step + n, n)
        copy = pltpu.make_async_remote_copy(
            src_ref=src,
            dst_ref=dst,
            send_sem=send_sem.at[slot],
            recv_sem=recv_sem.at[slot],
            device_id={AXES[axis]: target},
            device_id_type=pl.DeviceIdType.MESH,
        )
        to = has_hi[axis] if up else has_lo[axis]
        fro = has_lo[axis] if up else has_hi[axis]

        @pl.when(to)
        def _():
            copy.start()

        def wait_recv():
            @pl.when(fro)
            def _():
                copy.wait_recv()

        pending.append((axis, up, copy))
        return wait_recv

    def over(body, group=None):
        xs = tuple(range(X)) if group is None else group

        def one(j, carry):
            y0 = pl.multiple_of(j * ROWS, ROWS)
            for x in xs:
                body(x, y0)
            return carry

        lax.fori_loop(0, chunks, one, 0)

    def pack_z(r, which, x, y0, value, first, up=True, down=True):
        k = which * X + x
        rows = pl.ds(y0, ROWS)
        for side, wanted, shift in ((0, up, (k + 1) % Z), (1, down, k)):
            if wanted:
                moved = pltpu.roll(value, shift, 1) if shift else value
                if not first:
                    moved = jnp.where(lane == k, moved, zsend[r, side, rows])
                zsend[r, side, rows] = moved

    def from_z(r, which, x, y0, value, lo=True, hi=True):
        k = which * X + x
        rows = pl.ds(y0, ROWS)
        zm = zp = None
        if lo:
            edge = zrecv[r, 0, rows]
            edge = pltpu.roll(edge, Z - k, 1) if k else edge
            zm = jnp.where(lane == 0, edge, pltpu.roll(value, 1, 1))
        if hi:
            zp = jnp.where(
                lane == Z - 1,
                pltpu.roll(zrecv[r, 1, rows], Z - 1 - k, 1),
                pltpu.roll(value, Z - 1, 1),
            )
        return zm, zp

    def send_y(r, refs, ups, downs):
        for f, ref in enumerate(refs):
            for x in range(X):
                k = f * X + x
                if f < ups:
                    ysend[r, 0, k : k + 1] = ref(x)[TOP + Y - 1 : TOP + Y]
                if f < downs:
                    ysend[r, 1, k : k + 1] = ref(x)[TOP : TOP + 1]
        waits = []
        for side, count, up in ((0, ups, True), (1, downs, False)):
            if count:
                waits.append(send(1, up, ysend.at[r, side], yrecv.at[r, side]))
        return waits

    def unpack_y(r, refs, ups, downs):
        for f, ref in enumerate(refs):
            for x in range(X):
                k = f * X + x
                if f < ups:
                    ref(x)[TOP - 1 : TOP] = yrecv[r, 0, k : k + 1]
                if f < downs:
                    ref(x)[TOP + Y : TOP + Y + 1] = yrecv[r, 1, k : k + 1]

    def send_z(r, up=True, down=True):
        waits = []
        if up:
            waits.append(send(2, True, zsend.at[r, 0], zrecv.at[r, 0]))
        if down:
            waits.append(send(2, False, zsend.at[r, 1], zrecv.at[r, 1]))
        return waits

    outer = (0,) if X == 1 else (0, X - 1)
    inner = tuple(range(1, X - 1))

    def begin(x, y0):
        rows, prow = pl.ds(y0, ROWS), pl.ds(y0 + TOP, ROWS)
        tissue = tissue_in[x, rows]
        u, c, d = u_in[x, rows], c_in[x, rows], d_in[x, rows]
        along = jnp.where(tissue == 0, 0.1, jnp.where(tissue == 1, 1.0, 1.5))
        across = jnp.where(tissue == 0, 0.1, jnp.where(tissue == 1, 1.0, 0.75))
        cx, dx = across * c, across * d
        pot[0, 0, x + 1, prow] = u
        kal[0, x + 1, rows] = along * c
        kal[1, x + 1, rows] = along * d
        kac[0, x, prow] = cx
        kac[1, x, prow] = dx
        cd[0, x + 1, prow] = c
        cd[1, x + 1, prow] = d
        for f, value in enumerate((u, cx, dx, c, d)):
            pack_z(0, f, x, y0, value, x == 0 and f == 0, up=f < 3)

    for load in loads[:4]:
        load.wait()
    over(begin, outer)
    pl.semaphore_wait(barrier, sum(n - 1 for n in sizes))
    waits = [
        send(0, True, pot.at[0, 0, X, blk], pot.at[0, 0, 0, blk]),
        send(0, False, pot.at[0, 0, 1, blk], pot.at[0, 0, X + 1, blk]),
        send(0, True, kal.at[:, X], kal.at[:, 0]),
        send(0, False, kal.at[:, 1], kal.at[:, X + 1]),
    ]
    over(begin, inner)
    refs0 = (
        lambda x: pot.at[0, 0, x + 1],
        lambda x: kac.at[0, x],
        lambda x: kac.at[1, x],
        lambda x: cd.at[0, x + 1],
        lambda x: cd.at[1, x + 1],
    )
    waits += send_y(0, refs0, 3, 5)
    waits += send_z(0)
    late = [send(0, False, cd.at[:, 1, blk], cd.at[:, X + 1, blk])]

    def clear(axis, lo, refs):
        @pl.when(jnp.logical_not(has_lo[axis] if lo else has_hi[axis]))
        def _():
            for ref in refs:
                ref[...] = jnp.zeros(ref.shape, F32)

    for lo, p in ((True, 0), (False, X + 1)):
        clear(0, lo, [pot.at[:, :, p], adj.at[:, p], kal.at[:, p]])
    clear(0, False, [cd.at[:, X + 1]])
    clear(0, True, [qx.at[0]])
    for lo, side in ((True, 0), (False, 1)):
        clear(1, lo, [yrecv.at[:, side]])
        clear(2, lo, [zrecv.at[:, side]])

    for load in loads[4:]:
        load.wait()

    sx, sy, sz, ss = sx_in[...], sy_in[...], sz_in[...], ss_in[...]
    sites = sx.shape[1]
    ys = place[1] * Y + lax.broadcasted_iota(jnp.int32, (Y, sites), 0)
    zs = place[2] * Z + lax.broadcasted_iota(jnp.int32, (Z, sites), 0)
    near_y = (jnp.abs(ys - sy) <= 1).astype(F32)
    near_z = (jnp.abs(zs - sz) <= 1).astype(F32)
    for t in range(STEPS - 1):
        for x in range(X):
            near_x = jnp.where(ss == t, (jnp.abs(place[0] * X + x - sx) <= 1).astype(F32), 0.0)
            stim[t, x] = lax.dot_general(
                near_y * near_x, near_z, (((1,), (1,)), ((), ())), preferred_element_type=F32
            )

    def local_forward(t):
        last = t == STEPS - 1

        def body(x, y0):
            rows, prow = pl.ds(y0, ROWS), pl.ds(y0 + TOP, ROWS)
            u = pot[t, 0, x + 1, prow]
            if t == 0:
                v, w = v_in[x, rows], w_in[x, rows]
            else:
                v, w = gates[t, 0, x, rows], gates[t, 1, x, rows]
            n = None if last else stim[t, x, rows]
            e = react(u, v, w, n, not last, t > 0, 0 < t < STEPS - 1)
            if not last:
                local[0, x, rows] = e["u"]
                gates[t + 1, 0, x, rows] = e["v"]
                gates[t + 1, 1, x, rows] = e["w"]
            if t > 0:
                du = pot[t, 1, x + 1, prow]
                dlocal = e["uu"] * du
                jac[t, 0, x, rows] = e["uu"]
                if t > 1:
                    dv, dw = dgates[t, 0, x, rows], dgates[t, 1, x, rows]
                    dlocal = dlocal + e["uv"] * dv + e["uw"] * dw
                    jac[t, 1, x, rows] = e["uv"]
                    jac[t, 2, x, rows] = e["uw"]
                local[1, x, rows] = dlocal
                if not last:
                    jac[t, 3, x, rows] = e["vu"]
                    jac[t, 4, x, rows] = e["wu"]
                    new_dv, new_dw = e["vu"] * du, e["wu"] * du
                    if t > 1:
                        jac[t, 5, x, rows] = e["vv"]
                        jac[t, 6, x, rows] = e["ww"]
                        new_dv = new_dv + e["vv"] * dv
                        new_dw = new_dw + e["ww"] * dw
                    dgates[t + 1, 0, x, rows] = new_dv
                    dgates[t + 1, 1, x, rows] = new_dw

        over(body)

    def neighbours(ref, r, which, x, y0):
        value = ref[x + 1, pl.ds(y0 + TOP, ROWS)]
        zm, zp = from_z(r, which, x, y0, value)
        return value, (
            ref[x, pl.ds(y0 + TOP, ROWS)],
            ref[x + 2, pl.ds(y0 + TOP, ROWS)],
            ref[x + 1, pl.ds(y0 + TOP - 1, ROWS)],
            ref[x + 1, pl.ds(y0 + TOP + 1, ROWS)],
            zm,
            zp,
        )

    def face_weights(x, y0):
        rows, prow = pl.ds(y0, ROWS), pl.ds(y0 + TOP, ROWS)
        live = (
            lo_flag[0] if x == 0 else None,
            hi_flag[0] if x == X - 1 else None,
            jnp.where(y0 + row == 0, lo_flag[1], 1.0),
            jnp.where(y0 + row == Y - 1, hi_flag[1], 1.0),
            jnp.where(lane == 0, lo_flag[2], 1.0),
            jnp.where(lane == Z - 1, hi_flag[2], 1.0),
        )
        weights = []
        for f in range(2):
            own = kal[f, x + 1, rows]
            mine = kac[f, x, prow]
            zm, zp = from_z(0, 1 + f, x, y0, mine)
            raw = (
                own + kal[f, x, rows],
                own + kal[f, x + 2, rows],
                mine + kac[f, x, pl.ds(y0 + TOP - 1, ROWS)],
                mine + kac[f, x, pl.ds(y0 + TOP + 1, ROWS)],
                mine + zm,
                mine + zp,
            )
            out = []
            for i in range(6):
                weight = 0.5 * raw[i]
                if live[i] is not None:
                    weight = weight * live[i]
                face[f, i, x, rows] = weight
                out.append(weight)
            weights.append(out)
        return weights

    def dot6(weights, diffs):
        return (weights[0] * diffs[0] + weights[1] * diffs[1]) + (
            (weights[2] * diffs[2] + weights[3] * diffs[3])
            + (weights[4] * diffs[4] + weights[5] * diffs[5])
        )

    def stencil_forward(t):
        last = t == STEPS - 1

        def body(x, y0):
            rows, prow = pl.ds(y0, ROWS), pl.ds(y0 + TOP, ROWS)
            u, around = neighbours(pot.at[t, 0], t, 0, x, y0)
            diffs = [value - u for value in around]
            zdiff[t, 0, x, rows] = diffs[4]
            zdiff[t, 1, x, rows] = diffs[5]
            if t == 0:
                wc, wd = face_weights(x, y0)
            else:
                wc = [face[0, i, x, rows] for i in range(6)]
                wd = [face[1, i, x, rows] for i in range(6)]
            new_du = dot6(wd, diffs)
            if t > 0:
                du, around = neighbours(pot.at[t, 1], t, 1, x, y0)
                new_du = new_du + local[1, x, rows] + dot6(wc, [value - du for value in around])
            obs = obs_in[x, rows]
            weighted = obs * new_du
            if t == 0:
                sums[0, :, :] += obs
            sums[1, :, :] += weighted * new_du
            if last:
                adj[t, x + 1, prow] = weighted
                pack_z(t + 1, 0, x, y0, weighted, x == 0)
            else:
                new_u = local[0, x, rows] + dot6(wc, diffs)
                pot[t + 1, 0, x + 1, prow] = new_u
                pot[t + 1, 1, x + 1, prow] = new_du
                pack_z(t + 1, 0, x, y0, new_u, x == 0)
                pack_z(t + 1, 1, x, y0, new_du, False)

        return body

    def send_x_adj(t):
        return [
            send(0, True, adj.at[t, X, blk], adj.at[t, 0, blk]),
            send(0, False, adj.at[t, 1, blk], adj.at[t, X + 1, blk]),
        ]

    def send_x_pot(t):
        return [
            send(0, True, pot.at[t, :, X, blk], pot.at[t, :, 0, blk]),
            send(0, False, pot.at[t, :, 1, blk], pot.at[t, :, X + 1, blk]),
        ]

    def prior_flux():
        def body(x, y0):
            rows, prow = pl.ds(y0, ROWS), pl.ds(y0 + TOP, ROWS)
            live_y = jnp.where(y0 + row == Y - 1, hi_flag[1], 1.0)
            live_z = jnp.where(lane == Z - 1, hi_flag[2], 1.0)
            steps = []
            for f in range(2):
                own = cd[f, x + 1, prow]
                dx = cd[f, x + 2, prow] - own
                if x == X - 1:
                    dx = dx * hi_flag[0]
                dy = (cd[f, x + 1, pl.ds(y0 + TOP + 1, ROWS)] - own) * live_y
                dz = (from_z(0, 3 + f, x, y0, own, lo=False)[1] - own) * live_z
                steps.append((dx, dy, dz))
            (a, b, c), (p, q, r) = steps
            m = lax.rsqrt(a * a + b * b + c * c + tv_smooth * tv_smooth)
            sums[2, :, :] += m * (p * p + q * q + r * r)
            qx[x + 1, rows] = m * p
            qy[x, prow] = m * q
            flux = m * r
            qz[x, rows] = flux
            pack_z(2 * STEPS, 0, x, y0, flux, x == 0, down=False)

        over(body)

    sums[...] = jnp.zeros(sums.shape, F32)
    refs_u = lambda t: (lambda x: pot.at[t, 0, x + 1], lambda x: pot.at[t, 1, x + 1])
    refs_a = lambda t: (lambda x: adj.at[t, x + 1],)
    refs_q = (lambda x: qy.at[x],)
    qr = 2 * STEPS
    for t in range(STEPS):
        local_forward(t)
        if t == 1:
            for wait in late:
                wait()
            prior_flux()
        for wait in waits:
            wait()
        if t == 0:
            unpack_y(0, refs0, 3, 5)
        else:
            unpack_y(t, refs_u(t), 2, 2)
        body = stencil_forward(t)
        over(body, outer)
        if t == STEPS - 1:
            waits = send_x_adj(t)
            over(body, inner)
            waits += send_y(t + 1, refs_a(t), 1, 1)
            waits += send_z(t + 1)
        else:
            waits = send_x_pot(t + 1)
            over(body, inner)
            waits += send_y(t + 1, refs_u(t + 1), 2, 2)
            waits += send_z(t + 1)
        if t == 1:
            late = [send(0, True, qx.at[X], qx.at[0])]
            late += send_y(qr, refs_q, 1, 0)
            late += send_z(qr, down=False)

    red_bufs = (red_x, red_y, red_z)
    red_base = (0, sizes[0] - 1, sizes[0] + sizes[1] - 2)

    def reduce_start(axis, value):
        n, buf, me = sizes[axis], red_bufs[axis], place[axis]
        red_own[axis] = value
        buf[pl.ds(me, 1)] = value[None]
        waits = []
        for k in range(1, n):
            slot = red_base[axis] + k - 1
            copy = pltpu.make_async_remote_copy(
                src_ref=red_own.at[axis],
                dst_ref=buf.at[me],
                send_sem=rsend_sem.at[slot],
                recv_sem=rrecv_sem.at[slot],
                device_id={AXES[axis]: lax.rem(me + k, n)},
                device_id_type=pl.DeviceIdType.MESH,
            )
            copy.start()
            pending.append((None, None, copy))
            arrival = pltpu.make_async_remote_copy(
                src_ref=red_own.at[axis],
                dst_ref=buf.at[lax.rem(me + n - k, n)],
                send_sem=rsend_sem.at[slot],
                recv_sem=rrecv_sem.at[slot],
                device_id={AXES[axis]: lax.rem(me + k, n)},
                device_id_type=pl.DeviceIdType.MESH,
            )
            waits.append(arrival.wait_recv)
        return waits

    def reduce_end(axis, waits):
        for wait in waits:
            wait()
        total = red_bufs[axis][0]
        for i in range(1, sizes[axis]):
            total = total + red_bufs[axis][i]
        return total

    part_row = lax.broadcasted_iota(jnp.int32, (8, Z), 0)
    parts = jnp.zeros((8, Z), F32)
    for i in range(3):
        parts = parts + jnp.where(part_row == i, jnp.sum(sums[i], axis=0, keepdims=True), 0.0)
    reduced = reduce_start(2, parts)

    def local_backward(t):
        def body(x, y0):
            rows, prow = pl.ds(y0, ROWS), pl.ds(y0 + TOP, ROWS)
            a = adj[t, x + 1, prow]
            new = jac[t, 0, x, rows] * a
            if t < STEPS - 1:
                b, c = bgates[t + 1, 0, x, rows], bgates[t + 1, 1, x, rows]
                new = new + jac[t, 3, x, rows] * b + jac[t, 4, x, rows] * c
            local[0, x, rows] = new + obs_in[x, rows] * pot[t, 1, x + 1, prow]
            if t > 1:
                new_b = jac[t, 1, x, rows] * a
                new_c = jac[t, 2, x, rows] * a
                if t < STEPS - 1:
                    new_b = new_b + jac[t, 5, x, rows] * b
                    new_c = new_c + jac[t, 6, x, rows] * c
                bgates[t, 0, x, rows] = new_b
                bgates[t, 1, x, rows] = new_c

        over(body)

    def stencil_backward(t):
        def body(x, y0):
            rows, prow = pl.ds(y0, ROWS), pl.ds(y0 + TOP, ROWS)
            a, around = neighbours(adj.at[t], STEPS + (STEPS - 1 - t), 0, x, y0)
            diffs = [value - a for value in around]
            if t > 0:
                wc = [face[0, i, x, rows] for i in range(6)]
                new = local[0, x, rows] + dot6(wc, diffs)
                adj[t - 1, x + 1, prow] = new
                pack_z(STEPS + (STEPS - t), 0, x, y0, new, x == 0)
            ref = pot.at[t, 0]
            u = ref[x + 1, prow]
            px = (ref[x, prow] - u) * diffs[0] * (lo_flag[0] if x == 0 else 1.0)
            px = px + (ref[x + 2, prow] - u) * diffs[1] * (hi_flag[0] if x == X - 1 else 1.0)
            live = [
                jnp.where(y0 + row == 0, lo_flag[1], 1.0),
                jnp.where(y0 + row == Y - 1, hi_flag[1], 1.0),
                jnp.where(lane == 0, lo_flag[2], 1.0),
                jnp.where(lane == Z - 1, hi_flag[2], 1.0),
            ]
            u_diffs = [
                ref[x + 1, pl.ds(y0 + TOP - 1, ROWS)] - u,
                ref[x + 1, pl.ds(y0 + TOP + 1, ROWS)] - u,
                zdiff[t, 0, x, rows],
                zdiff[t, 1, x, rows],
            ]
            pyz = sum(u_diffs[i] * diffs[2 + i] * live[i] for i in range(4))
            tissue = tissue_in[x, rows]
            along = jnp.where(tissue == 0, -0.05, jnp.where(tissue == 1, -0.5, -0.75))
            across = jnp.where(tissue == 0, -0.05, jnp.where(tissue == 1, -0.5, -0.375))
            term = along * px + across * pyz
            if t < STEPS - 1:
                term = term + grad[x, rows]
            grad[x, rows] = term

        return body

    for t in reversed(range(STEPS)):
        r = STEPS + (STEPS - 1 - t)
        if t > 0:
            local_backward(t)
        for wait in waits:
            wait()
        unpack_y(r, refs_a(t), 1, 1)
        body = stencil_backward(t)
        over(body, outer)
        if t > 0:
            waits = send_x_adj(t - 1)
            over(body, inner)
            waits += send_y(r + 1, refs_a(t - 1), 1, 1)
            waits += send_z(r + 1)
            if t == STEPS - 1:
                reduced = reduce_start(1, reduce_end(2, reduced))
            if t == STEPS - 2:
                reduced = reduce_start(0, reduce_end(1, reduced))
        else:
            over(body, inner)
    total = reduce_end(0, reduced)

    for wait in late:
        wait()
    unpack_y(qr, refs_q, 1, 0)
    voxels = float(X * sizes[0]) * float(Y * sizes[1]) * float(Z * sizes[2])
    factor = voxels / jnp.sum(total[0:1], axis=1, keepdims=True)
    misfit = jnp.sum(total[1:2], axis=1, keepdims=True)
    smooth = jnp.sum(total[2:3], axis=1, keepdims=True)
    curv_out[...] = factor * misfit + tv_weight * smooth

    def finish(x, y0):
        rows, prow = pl.ds(y0, ROWS), pl.ds(y0 + TOP, ROWS)
        here = qz[x, rows]
        prior = (
            (qx[x, rows] - qx[x + 1, rows])
            + (qy[x, pl.ds(y0 + TOP - 1, ROWS)] - qy[x, prow])
            + (from_z(qr, 0, x, y0, here, hi=False)[0] - here)
        )
        hess_out[x, rows] = grad[x, rows] * factor + tv_weight * prior

    over(finish)
    for axis in (0, 1, 2, None):
        for up in (True, False):
            mine = [c for a, b, c in pending if a == axis and (axis is None or b == up)]
            if axis is None:
                if up:
                    for copy in mine:
                        copy.wait_send()
                continue

            @pl.when(has_hi[axis] if up else has_lo[axis])
            def _():
                for copy in mine:
                    copy.wait_send()


def shards(sizes, *args):
    X, Y, Z = args[0].shape
    dense = lambda *lead: pltpu.VMEM((*lead, Y, Z), F32)
    tall = lambda *lead: pltpu.VMEM((*lead, Y + 2 * TOP, Z), F32)
    lines = sum(n - 1 for n in sizes)
    rounds = 2 * STEPS + 1
    face_rows = -(-5 * X // 8) * 8
    copies = 9 + 6 * (STEPS - 1) + 6 * STEPS + 3
    vmem = pl.BlockSpec(memory_space=pltpu.VMEM)
    stims = [a.reshape(1, a.shape[0]) for a in args[7:]]
    hess, curv = pl.pallas_call(
        partial(kernel, sizes),
        out_shape=(
            jax.ShapeDtypeStruct((X, Y, Z), F32),
            jax.ShapeDtypeStruct((1, 1), F32),
        ),
        in_specs=[pl.BlockSpec(memory_space=pltpu.HBM)] * 11,
        out_specs=(vmem, vmem),
        scratch_shapes=[pltpu.VMEM(a.shape, a.dtype) for a in (*args[:7], *stims)]
        + [
            tall(STEPS, 2, X + 2),
            tall(STEPS, X + 2),
            dense(2, X + 2),
            tall(2, X),
            tall(2, X + 2),
            dense(2, 6, X),
            dense(STEPS, 2, X),
            dense(STEPS, 2, X),
            dense(STEPS, 2, X),
            dense(STEPS, 7, X),
            dense(2, X),
            dense(STEPS - 1, X),
            dense(STEPS, 2, X),
            dense(X),
            dense(X + 1),
            tall(X),
            dense(X),
            pltpu.VMEM((3, ROWS, Z), F32),
            dense(rounds, 2),
            dense(rounds, 2),
            pltpu.VMEM((rounds, 2, face_rows, Z), F32),
            pltpu.VMEM((rounds, 2, face_rows, Z), F32),
            pltpu.VMEM((3, 8, Z), F32),
            pltpu.VMEM((sizes[0], 8, Z), F32),
            pltpu.VMEM((sizes[1], 8, Z), F32),
            pltpu.VMEM((sizes[2], 8, Z), F32),
            pltpu.SemaphoreType.DMA((copies,)),
            pltpu.SemaphoreType.DMA((copies,)),
            pltpu.SemaphoreType.DMA((lines,)),
            pltpu.SemaphoreType.DMA((lines,)),
            pltpu.SemaphoreType.DMA((11,)),
        ],
        compiler_params=pltpu.CompilerParams(
            collective_id=0, has_side_effects=True, vmem_limit_bytes=56 * 1024 * 1024
        ),
    )(*args[:7], *stims)
    return hess, curv.reshape(())


def solution(mesh):
    sizes = tuple(mesh.shape[a] for a in AXES)
    split = P(*AXES)
    return jax.shard_map(
        partial(shards, sizes),
        mesh=mesh,
        in_specs=(split,) * 7 + (P(),) * 4,
        out_specs=(split, P()),
        check_vma=False,
    )
```

```python
from functools import partial

import jax
import jax.numpy as jnp
from jax import lax
from jax.experimental import pallas as pl
from jax.experimental.pallas import tpu as pltpu
from jax.sharding import PartitionSpec as P

STEPS = 4
AXES = ("gx", "gy", "gz")

time_step = 0.25
u_crit = 0.13
u_gate = 0.04
switch_width = 0.05
tau_fast = 0.4
tau_open = 12.5
tau_repol = 33.33
tau_slow = 15.0
k_slow = 10.0
u_slow = 0.85
tau_vplus = 3.33
tau_vminus_one = 19.6
tau_vminus_two = 1000.0
tau_wplus = 667.0
tau_wminus = 11.0
stim_amp = 2.0
tv_weight = 0.05
tv_smooth = 0.02

ROWS = 64
TOP = 8
F32 = jnp.float32


def react(u, v, w, stim, primal, jac_u, jac_gates):
    out = {}
    opened = 0.5 * (1.0 + jnp.tanh((u - u_crit) * (1.0 / switch_width)))
    closed = 1.0 - opened
    slow = jnp.tanh(k_slow * (u - u_slow))
    hump = (1.0 - u) * (u - u_crit)
    uv = (time_step / tau_fast) * opened * hump
    uw = (time_step / (2.0 * tau_slow)) * (1.0 + slow)
    if primal:
        slow_out = u * closed * (1.0 / tau_open) + opened * (1.0 / tau_repol)
        out["u"] = u + (time_step * stim_amp) * stim + v * uv + w * uw - time_step * slow_out
    if jac_u or jac_gates:
        d_open = (2.0 / switch_width) * opened * closed
    if jac_u:
        d_hump = (1.0 + u_crit) - 2.0 * u
        d_fast = v * (1.0 / tau_fast) * (d_open * hump + opened * d_hump)
        d_out = closed * (1.0 / tau_open) + d_open * (1.0 / tau_repol - u * (1.0 / tau_open))
        d_in = w * (k_slow / (2.0 * tau_slow)) * (1.0 - slow * slow)
        out["uu"] = 1.0 + time_step * (d_fast - d_out + d_in)
        out["uv"] = uv
        out["uw"] = uw
    if primal or jac_gates:
        partly = 0.5 * (1.0 + jnp.tanh((u - u_gate) * (1.0 / switch_width)))
        slowness = 1.0 / (partly * tau_vminus_one + (1.0 - partly) * tau_vminus_two)
        keep_v = jnp.exp(-time_step * (opened * (1.0 / tau_vplus) + closed * slowness))
        keep_w = jnp.exp(-time_step * (opened * (1.0 / tau_wplus) + closed * (1.0 / tau_wminus)))
        far_v = (v - closed) * keep_v
        far_w = (w - closed) * keep_w
        out["v"] = closed + far_v
        out["w"] = closed + far_w
        out["vv"] = keep_v
        out["ww"] = keep_w
    if jac_gates:
        d_partly = (2.0 / switch_width) * partly * (1.0 - partly)
        d_rate_v = d_open * (1.0 / tau_vplus - slowness) + closed * d_partly * (
            (tau_vminus_two - tau_vminus_one) * slowness * slowness
        )
        d_rate_w = d_open * (1.0 / tau_wplus - 1.0 / tau_wminus)
        out["vu"] = d_open * (keep_v - 1.0) - time_step * far_v * d_rate_v
        out["wu"] = d_open * (keep_w - 1.0) - time_step * far_w * d_rate_w
    return out


def kernel(
    sizes,
    u_hbm,
    v_hbm,
    w_hbm,
    c_hbm,
    d_hbm,
    obs_hbm,
    tissue_hbm,
    sx_hbm,
    sy_hbm,
    sz_hbm,
    ss_hbm,
    hess_out,
    curv_out,
    u_in,
    v_in,
    w_in,
    c_in,
    d_in,
    obs_in,
    tissue_in,
    sx_in,
    sy_in,
    sz_in,
    ss_in,
    pot,
    adj,
    kal,
    kac,
    cd,
    face,
    gates,
    dgates,
    bgates,
    jac,
    local,
    stim,
    zdiff,
    grad,
    qx,
    qy,
    qz,
    sums,
    zsend,
    zrecv,
    ysend,
    yrecv,
    red_own,
    red_x,
    red_y,
    red_z,
    send_sem,
    recv_sem,
    rsend_sem,
    rrecv_sem,
    load_sem,
):
    pairs = (
        (tissue_hbm, tissue_in),
        (u_hbm, u_in),
        (c_hbm, c_in),
        (d_hbm, d_in),
        (sx_hbm, sx_in),
        (sy_hbm, sy_in),
        (sz_hbm, sz_in),
        (ss_hbm, ss_in),
        (v_hbm, v_in),
        (w_hbm, w_in),
        (obs_hbm, obs_in),
    )
    loads = [pltpu.make_async_copy(a, b, load_sem.at[i]) for i, (a, b) in enumerate(pairs)]
    for load in loads:
        load.start()
    X, Y, Z = u_in.shape
    chunks = Y // ROWS
    place = [lax.axis_index(a) for a in AXES]
    has_lo = [p > 0 for p in place]
    has_hi = [p < n - 1 for p, n in zip(place, sizes)]
    lo_flag = [h.astype(F32) for h in has_lo]
    hi_flag = [h.astype(F32) for h in has_hi]

    barrier = pltpu.get_barrier_semaphore()
    for a, n in enumerate(sizes):
        for k in range(1, n):
            pl.semaphore_signal(
                barrier,
                inc=1,
                device_id={AXES[a]: lax.rem(place[a] + k, n)},
                device_id_type=pl.DeviceIdType.MESH,
            )

    lane = lax.broadcasted_iota(jnp.int32, (ROWS, Z), 1)
    row = lax.broadcasted_iota(jnp.int32, (ROWS, Z), 0)
    blk = pl.ds(TOP, Y)

    pending = []
    counter = [0]

    def send(axis, up, src, dst):
        slot = counter[0]
        counter[0] += 1
        step = 1 if up else -1
        n = sizes[axis]
        target = lax.rem(place[axis] + step + n, n)
        copy = pltpu.make_async_remote_copy(
            src_ref=src,
            dst_ref=dst,
            send_sem=send_sem.at[slot],
            recv_sem=recv_sem.at[slot],
            device_id={AXES[axis]: target},
            device_id_type=pl.DeviceIdType.MESH,
        )
        to = has_hi[axis] if up else has_lo[axis]
        fro = has_lo[axis] if up else has_hi[axis]

        @pl.when(to)
        def _():
            copy.start()

        def wait_recv():
            @pl.when(fro)
            def _():
                copy.wait_recv()

        pending.append((axis, up, copy))
        return wait_recv

    def over(body, group=None):
        xs = tuple(range(X)) if group is None else group

        def one(j, carry):
            y0 = pl.multiple_of(j * ROWS, ROWS)
            for x in xs:
                body(x, y0)
            return carry

        lax.fori_loop(0, chunks, one, 0)

    def pack_z(r, which, x, y0, value, first, up=True, down=True):
        k = which * X + x
        rows = pl.ds(y0, ROWS)
        for side, wanted, shift in ((0, up, (k + 1) % Z), (1, down, k)):
            if wanted:
                moved = pltpu.roll(value, shift, 1) if shift else value
                if not first:
                    moved = jnp.where(lane == k, moved, zsend[r, side, rows])
                zsend[r, side, rows] = moved

    def from_z(r, which, x, y0, value, lo=True, hi=True):
        k = which * X + x
        rows = pl.ds(y0, ROWS)
        zm = zp = None
        if lo:
            edge = zrecv[r, 0, rows]
            edge = pltpu.roll(edge, Z - k, 1) if k else edge
            zm = jnp.where(lane == 0, edge, pltpu.roll(value, 1, 1))
        if hi:
            zp = jnp.where(
                lane == Z - 1,
                pltpu.roll(zrecv[r, 1, rows], Z - 1 - k, 1),
                pltpu.roll(value, Z - 1, 1),
            )
        return zm, zp

    def send_y(r, refs, ups, downs):
        for f, ref in enumerate(refs):
            for x in range(X):
                k = f * X + x
                if f < ups:
                    ysend[r, 0, k : k + 1] = ref(x)[TOP + Y - 1 : TOP + Y]
                if f < downs:
                    ysend[r, 1, k : k + 1] = ref(x)[TOP : TOP + 1]
        waits = []
        for side, count, up in ((0, ups, True), (1, downs, False)):
            if count:
                used = pl.ds(0, -(-count * X // 8) * 8)
                waits.append(send(1, up, ysend.at[r, side, used], yrecv.at[r, side, used]))
        return waits

    def unpack_y(r, refs, ups, downs):
        for f, ref in enumerate(refs):
            for x in range(X):
                k = f * X + x
                if f < ups:
                    ref(x)[TOP - 1 : TOP] = yrecv[r, 0, k : k + 1]
                if f < downs:
                    ref(x)[TOP + Y : TOP + Y + 1] = yrecv[r, 1, k : k + 1]

    def send_z(r, up=True, down=True):
        waits = []
        if up:
            waits.append(send(2, True, zsend.at[r, 0], zrecv.at[r, 0]))
        if down:
            waits.append(send(2, False, zsend.at[r, 1], zrecv.at[r, 1]))
        return waits

    outer = (0,) if X == 1 else (0, X - 1)
    inner = tuple(range(1, X - 1))

    def begin(x, y0):
        rows, prow = pl.ds(y0, ROWS), pl.ds(y0 + TOP, ROWS)
        tissue = tissue_in[x, rows]
        u, c, d = u_in[x, rows], c_in[x, rows], d_in[x, rows]
        along = jnp.where(tissue == 0, 0.1, jnp.where(tissue == 1, 1.0, 1.5))
        across = jnp.where(tissue == 0, 0.1, jnp.where(tissue == 1, 1.0, 0.75))
        cx, dx = across * c, across * d
        pot[0, 0, x + 1, prow] = u
        kal[0, x + 1, rows] = along * c
        kal[1, x + 1, rows] = along * d
        kac[0, x, prow] = cx
        kac[1, x, prow] = dx
        cd[0, x + 1, prow] = c
        cd[1, x + 1, prow] = d
        for f, value in enumerate((u, cx, dx, c, d)):
            pack_z(0, f, x, y0, value, x == 0 and f == 0, up=f < 3)

    for load in loads[:4]:
        load.wait()
    over(begin, outer)
    pl.semaphore_wait(barrier, sum(n - 1 for n in sizes))
    waits = [
        send(0, True, pot.at[0, 0, X, blk], pot.at[0, 0, 0, blk]),
        send(0, False, pot.at[0, 0, 1, blk], pot.at[0, 0, X + 1, blk]),
        send(0, True, kal.at[:, X], kal.at[:, 0]),
        send(0, False, kal.at[:, 1], kal.at[:, X + 1]),
    ]
    over(begin, inner)
    refs0 = (
        lambda x: pot.at[0, 0, x + 1],
        lambda x: kac.at[0, x],
        lambda x: kac.at[1, x],
        lambda x: cd.at[0, x + 1],
        lambda x: cd.at[1, x + 1],
    )
    waits += send_y(0, refs0, 3, 5)
    waits += send_z(0)

    def clear(axis, lo, refs):
        @pl.when(jnp.logical_not(has_lo[axis] if lo else has_hi[axis]))
        def _():
            for ref in refs:
                ref[...] = jnp.zeros(ref.shape, F32)

    for lo, p in ((True, 0), (False, X + 1)):
        clear(0, lo, [pot.at[:, :, p], adj.at[:, p], kal.at[:, p]])
    clear(0, False, [cd.at[:, X + 1]])
    clear(0, True, [qx.at[0]])
    for lo, side in ((True, 0), (False, 1)):
        clear(1, lo, [yrecv.at[:, side]])
        clear(2, lo, [zrecv.at[:, side]])

    for load in loads[4:]:
        load.wait()

    sx, sy, sz, ss = sx_in[...], sy_in[...], sz_in[...], ss_in[...]
    sites = sx.shape[1]
    ys = place[1] * Y + lax.broadcasted_iota(jnp.int32, (Y, sites), 0)
    zs = place[2] * Z + lax.broadcasted_iota(jnp.int32, (Z, sites), 0)
    near_y = (jnp.abs(ys - sy) <= 1).astype(F32)
    near_z = (jnp.abs(zs - sz) <= 1).astype(F32)
    for t in range(STEPS - 1):
        for x in range(X):
            near_x = jnp.where(ss == t, (jnp.abs(place[0] * X + x - sx) <= 1).astype(F32), 0.0)
            stim[t, x] = lax.dot_general(
                near_y * near_x, near_z, (((1,), (1,)), ((), ())), preferred_element_type=F32
            )

    def local_forward(t):
        last = t == STEPS - 1

        def body(x, y0):
            rows, prow = pl.ds(y0, ROWS), pl.ds(y0 + TOP, ROWS)
            u = pot[t, 0, x + 1, prow]
            if t == 0:
                v, w = v_in[x, rows], w_in[x, rows]
            else:
                v, w = gates[t, 0, x, rows], gates[t, 1, x, rows]
            n = None if last else stim[t, x, rows]
            e = react(u, v, w, n, not last, t > 0, 0 < t < STEPS - 1)
            if not last:
                local[0, x, rows] = e["u"]
                gates[t + 1, 0, x, rows] = e["v"]
                gates[t + 1, 1, x, rows] = e["w"]
            if t > 0:
                du = pot[t, 1, x + 1, prow]
                dlocal = e["uu"] * du
                jac[t, 0, x, rows] = e["uu"]
                if t > 1:
                    dv, dw = dgates[t, 0, x, rows], dgates[t, 1, x, rows]
                    dlocal = dlocal + e["uv"] * dv + e["uw"] * dw
                    jac[t, 1, x, rows] = e["uv"]
                    jac[t, 2, x, rows] = e["uw"]
                local[1, x, rows] = dlocal
                if not last:
                    jac[t, 3, x, rows] = e["vu"]
                    jac[t, 4, x, rows] = e["wu"]
                    new_dv, new_dw = e["vu"] * du, e["wu"] * du
                    if t > 1:
                        jac[t, 5, x, rows] = e["vv"]
                        jac[t, 6, x, rows] = e["ww"]
                        new_dv = new_dv + e["vv"] * dv
                        new_dw = new_dw + e["ww"] * dw
                    dgates[t + 1, 0, x, rows] = new_dv
                    dgates[t + 1, 1, x, rows] = new_dw

        over(body)

    def neighbours(ref, r, which, x, y0):
        value = ref[x + 1, pl.ds(y0 + TOP, ROWS)]
        zm, zp = from_z(r, which, x, y0, value)
        return value, (
            ref[x, pl.ds(y0 + TOP, ROWS)],
            ref[x + 2, pl.ds(y0 + TOP, ROWS)],
            ref[x + 1, pl.ds(y0 + TOP - 1, ROWS)],
            ref[x + 1, pl.ds(y0 + TOP + 1, ROWS)],
            zm,
            zp,
        )

    def face_weights(x, y0):
        rows, prow = pl.ds(y0, ROWS), pl.ds(y0 + TOP, ROWS)
        live = (
            lo_flag[0] if x == 0 else None,
            hi_flag[0] if x == X - 1 else None,
            jnp.where(y0 + row == 0, lo_flag[1], 1.0),
            jnp.where(y0 + row == Y - 1, hi_flag[1], 1.0),
            jnp.where(lane == 0, lo_flag[2], 1.0),
            jnp.where(lane == Z - 1, hi_flag[2], 1.0),
        )
        weights = []
        for f in range(2):
            own = kal[f, x + 1, rows]
            mine = kac[f, x, prow]
            zm, zp = from_z(0, 1 + f, x, y0, mine)
            raw = (
                own + kal[f, x, rows],
                own + kal[f, x + 2, rows],
                mine + kac[f, x, pl.ds(y0 + TOP - 1, ROWS)],
                mine + kac[f, x, pl.ds(y0 + TOP + 1, ROWS)],
                mine + zm,
                mine + zp,
            )
            out = []
            for i in range(6):
                weight = 0.5 * raw[i]
                if live[i] is not None:
                    weight = weight * live[i]
                face[f, i, x, rows] = weight
                out.append(weight)
            weights.append(out)
        return weights

    def dot6(weights, diffs):
        return (weights[0] * diffs[0] + weights[1] * diffs[1]) + (
            (weights[2] * diffs[2] + weights[3] * diffs[3])
            + (weights[4] * diffs[4] + weights[5] * diffs[5])
        )

    def stencil_forward(t):
        last = t == STEPS - 1

        def body(x, y0):
            rows, prow = pl.ds(y0, ROWS), pl.ds(y0 + TOP, ROWS)
            u, around = neighbours(pot.at[t, 0], t, 0, x, y0)
            diffs = [value - u for value in around]
            zdiff[t, 0, x, rows] = diffs[4]
            zdiff[t, 1, x, rows] = diffs[5]
            if t == 0:
                wc, wd = face_weights(x, y0)
            else:
                wc = [face[0, i, x, rows] for i in range(6)]
                wd = [face[1, i, x, rows] for i in range(6)]
            new_du = dot6(wd, diffs)
            if t > 0:
                du, around = neighbours(pot.at[t, 1], t, 1, x, y0)
                new_du = new_du + local[1, x, rows] + dot6(wc, [value - du for value in around])
            obs = obs_in[x, rows]
            weighted = obs * new_du
            if t == 0:
                sums[0, :, :] += obs
            sums[1, :, :] += weighted * new_du
            if last:
                adj[t, x + 1, prow] = weighted
                pack_z(t + 1, 0, x, y0, weighted, x == 0)
            else:
                new_u = local[0, x, rows] + dot6(wc, diffs)
                pot[t + 1, 0, x + 1, prow] = new_u
                pot[t + 1, 1, x + 1, prow] = new_du
                pack_z(t + 1, 0, x, y0, new_u, x == 0)
                pack_z(t + 1, 1, x, y0, new_du, False)

        return body

    def send_x_adj(t):
        return [
            send(0, True, adj.at[t, X, blk], adj.at[t, 0, blk]),
            send(0, False, adj.at[t, 1, blk], adj.at[t, X + 1, blk]),
        ]

    def send_x_pot(t):
        return [
            send(0, True, pot.at[t, :, X, blk], pot.at[t, :, 0, blk]),
            send(0, False, pot.at[t, :, 1, blk], pot.at[t, :, X + 1, blk]),
        ]

    def prior_flux():
        def body(x, y0):
            rows, prow = pl.ds(y0, ROWS), pl.ds(y0 + TOP, ROWS)
            live_y = jnp.where(y0 + row == Y - 1, hi_flag[1], 1.0)
            live_z = jnp.where(lane == Z - 1, hi_flag[2], 1.0)
            steps = []
            for f in range(2):
                own = cd[f, x + 1, prow]
                dx = cd[f, x + 2, prow] - own
                if x == X - 1:
                    dx = dx * hi_flag[0]
                dy = (cd[f, x + 1, pl.ds(y0 + TOP + 1, ROWS)] - own) * live_y
                dz = (from_z(0, 3 + f, x, y0, own, lo=False)[1] - own) * live_z
                steps.append((dx, dy, dz))
            (a, b, c), (p, q, r) = steps
            m = lax.rsqrt(a * a + b * b + c * c + tv_smooth * tv_smooth)
            sums[2, :, :] += m * (p * p + q * q + r * r)
            qx[x + 1, rows] = m * p
            qy[x, prow] = m * q
            flux = m * r
            qz[x, rows] = flux
            pack_z(2 * STEPS, 0, x, y0, flux, x == 0, down=False)

        over(body)

    sums[...] = jnp.zeros(sums.shape, F32)
    refs_u = lambda t: (lambda x: pot.at[t, 0, x + 1], lambda x: pot.at[t, 1, x + 1])
    refs_a = lambda t: (lambda x: adj.at[t, x + 1],)
    refs_q = (lambda x: qy.at[x],)
    qr = 2 * STEPS
    for t in range(STEPS):
        local_forward(t)
        if t == 1:
            for wait in late:
                wait()
            prior_flux()
        for wait in waits:
            wait()
        if t == 0:
            late = [send(0, False, cd.at[:, 1, blk], cd.at[:, X + 1, blk])]
            unpack_y(0, refs0, 3, 5)
        else:
            unpack_y(t, refs_u(t), 2, 2)
        body = stencil_forward(t)
        over(body, outer)
        if t == STEPS - 1:
            waits = send_x_adj(t)
            over(body, inner)
            waits += send_y(t + 1, refs_a(t), 1, 1)
            waits += send_z(t + 1)
        else:
            waits = send_x_pot(t + 1)
            over(body, inner)
            waits += send_y(t + 1, refs_u(t + 1), 2, 2)
            waits += send_z(t + 1)
        if t == 1:
            late = [send(0, True, qx.at[X], qx.at[0])]
            late += send_y(qr, refs_q, 1, 0)
            late += send_z(qr, down=False)

    red_bufs = (red_x, red_y, red_z)
    red_base = (0, sizes[0] - 1, sizes[0] + sizes[1] - 2)

    def reduce_start(axis, value):
        n, buf, me = sizes[axis], red_bufs[axis], place[axis]
        red_own[axis] = value
        buf[pl.ds(me, 1)] = value[None]
        waits = []
        for k in range(1, n):
            slot = red_base[axis] + k - 1
            copy = pltpu.make_async_remote_copy(
                src_ref=red_own.at[axis],
                dst_ref=buf.at[me],
                send_sem=rsend_sem.at[slot],
                recv_sem=rrecv_sem.at[slot],
                device_id={AXES[axis]: lax.rem(me + k, n)},
                device_id_type=pl.DeviceIdType.MESH,
            )
            copy.start()
            pending.append((None, None, copy))
            arrival = pltpu.make_async_remote_copy(
                src_ref=red_own.at[axis],
                dst_ref=buf.at[lax.rem(me + n - k, n)],
                send_sem=rsend_sem.at[slot],
                recv_sem=rrecv_sem.at[slot],
                device_id={AXES[axis]: lax.rem(me + k, n)},
                device_id_type=pl.DeviceIdType.MESH,
            )
            waits.append(arrival.wait_recv)
        return waits

    def reduce_end(axis, waits):
        for wait in waits:
            wait()
        total = red_bufs[axis][0]
        for i in range(1, sizes[axis]):
            total = total + red_bufs[axis][i]
        return total

    part_row = lax.broadcasted_iota(jnp.int32, (8, Z), 0)
    parts = jnp.zeros((8, Z), F32)
    for i in range(3):
        parts = parts + jnp.where(part_row == i, jnp.sum(sums[i], axis=0, keepdims=True), 0.0)
    reduced = reduce_start(2, parts)

    def local_backward(t):
        def body(x, y0):
            rows, prow = pl.ds(y0, ROWS), pl.ds(y0 + TOP, ROWS)
            a = adj[t, x + 1, prow]
            new = jac[t, 0, x, rows] * a
            if t < STEPS - 1:
                b, c = bgates[t + 1, 0, x, rows], bgates[t + 1, 1, x, rows]
                new = new + jac[t, 3, x, rows] * b + jac[t, 4, x, rows] * c
            local[0, x, rows] = new + obs_in[x, rows] * pot[t, 1, x + 1, prow]
            if t > 1:
                new_b = jac[t, 1, x, rows] * a
                new_c = jac[t, 2, x, rows] * a
                if t < STEPS - 1:
                    new_b = new_b + jac[t, 5, x, rows] * b
                    new_c = new_c + jac[t, 6, x, rows] * c
                bgates[t, 0, x, rows] = new_b
                bgates[t, 1, x, rows] = new_c

        over(body)

    def stencil_backward(t):
        def body(x, y0):
            rows, prow = pl.ds(y0, ROWS), pl.ds(y0 + TOP, ROWS)
            a, around = neighbours(adj.at[t], STEPS + (STEPS - 1 - t), 0, x, y0)
            wc = [face[0, i, x, rows] for i in range(6)]
            new = local[0, x, rows] + dot6(wc, [value - a for value in around])
            adj[t - 1, x + 1, prow] = new
            pack_z(STEPS + (STEPS - t), 0, x, y0, new, x == 0)

        return body

    def gradient_of(t):
        def body(x, y0):
            rows, prow = pl.ds(y0, ROWS), pl.ds(y0 + TOP, ROWS)
            a, around = neighbours(adj.at[t], STEPS + (STEPS - 1 - t), 0, x, y0)
            diffs = [value - a for value in around]
            ref = pot.at[t, 0]
            u = ref[x + 1, prow]
            px = (ref[x, prow] - u) * diffs[0] * (lo_flag[0] if x == 0 else 1.0)
            px = px + (ref[x + 2, prow] - u) * diffs[1] * (hi_flag[0] if x == X - 1 else 1.0)
            live = [
                jnp.where(y0 + row == 0, lo_flag[1], 1.0),
                jnp.where(y0 + row == Y - 1, hi_flag[1], 1.0),
                jnp.where(lane == 0, lo_flag[2], 1.0),
                jnp.where(lane == Z - 1, hi_flag[2], 1.0),
            ]
            u_diffs = [
                ref[x + 1, pl.ds(y0 + TOP - 1, ROWS)] - u,
                ref[x + 1, pl.ds(y0 + TOP + 1, ROWS)] - u,
                zdiff[t, 0, x, rows],
                zdiff[t, 1, x, rows],
            ]
            pyz = sum(u_diffs[i] * diffs[2 + i] * live[i] for i in range(4))
            tissue = tissue_in[x, rows]
            along = jnp.where(tissue == 0, -0.05, jnp.where(tissue == 1, -0.5, -0.75))
            across = jnp.where(tissue == 0, -0.05, jnp.where(tissue == 1, -0.5, -0.375))
            term = along * px + across * pyz
            if t < STEPS - 1:
                term = term + grad[x, rows]
            if t > 0:
                grad[x, rows] = term
            else:
                hess_out[x, rows] = term * factor + hess_out[x, rows]

        over(body)

    def prior_of(x, y0):
        rows, prow = pl.ds(y0, ROWS), pl.ds(y0 + TOP, ROWS)
        here = qz[x, rows]
        hess_out[x, rows] = tv_weight * (
            (qx[x, rows] - qx[x + 1, rows])
            + (qy[x, pl.ds(y0 + TOP - 1, ROWS)] - qy[x, prow])
            + (from_z(qr, 0, x, y0, here, hi=False)[0] - here)
        )

    for t in reversed(range(STEPS)):
        r = STEPS + (STEPS - 1 - t)
        if t > 0:
            local_backward(t)
        if t < STEPS - 1:
            gradient_of(t + 1)
        if t == 0:
            total = reduce_end(0, reduced)
            voxels = float(X * sizes[0]) * float(Y * sizes[1]) * float(Z * sizes[2])
            factor = voxels / jnp.sum(total[0:1], axis=1, keepdims=True)
            misfit = jnp.sum(total[1:2], axis=1, keepdims=True)
            smooth = jnp.sum(total[2:3], axis=1, keepdims=True)
            curv_out[...] = factor * misfit + tv_weight * smooth
            for wait in late:
                wait()
            unpack_y(qr, refs_q, 1, 0)
            over(prior_of)
        for wait in waits:
            wait()
        unpack_y(r, refs_a(t), 1, 1)
        if t > 0:
            body = stencil_backward(t)
            over(body, outer)
            waits = send_x_adj(t - 1)
            over(body, inner)
            waits += send_y(r + 1, refs_a(t - 1), 1, 1)
            waits += send_z(r + 1)
            if t == STEPS - 1:
                reduced = reduce_start(1, reduce_end(2, reduced))
            if t == STEPS - 2:
                reduced = reduce_start(0, reduce_end(1, reduced))
        else:
            gradient_of(0)

    for axis in (0, 1, 2, None):
        for up in (True, False):
            mine = [c for a, b, c in pending if a == axis and (axis is None or b == up)]
            if axis is None:
                if up:
                    for copy in mine:
                        copy.wait_send()
                continue

            @pl.when(has_hi[axis] if up else has_lo[axis])
            def _():
                for copy in mine:
                    copy.wait_send()


def shards(sizes, *args):
    X, Y, Z = args[0].shape
    dense = lambda *lead: pltpu.VMEM((*lead, Y, Z), F32)
    tall = lambda *lead: pltpu.VMEM((*lead, Y + 2 * TOP, Z), F32)
    lines = sum(n - 1 for n in sizes)
    rounds = 2 * STEPS + 1
    face_rows = -(-5 * X // 8) * 8
    copies = 9 + 6 * (STEPS - 1) + 6 * STEPS + 3
    vmem = pl.BlockSpec(memory_space=pltpu.VMEM)
    stims = [a.reshape(1, a.shape[0]) for a in args[7:]]
    hess, curv = pl.pallas_call(
        partial(kernel, sizes),
        out_shape=(
            jax.ShapeDtypeStruct((X, Y, Z), F32),
            jax.ShapeDtypeStruct((1, 1), F32),
        ),
        in_specs=[pl.BlockSpec(memory_space=pltpu.HBM)] * 11,
        out_specs=(vmem, vmem),
        scratch_shapes=[pltpu.VMEM(a.shape, a.dtype) for a in (*args[:7], *stims)]
        + [
            tall(STEPS, 2, X + 2),
            tall(STEPS, X + 2),
            dense(2, X + 2),
            tall(2, X),
            tall(2, X + 2),
            dense(2, 6, X),
            dense(STEPS, 2, X),
            dense(STEPS, 2, X),
            dense(STEPS, 2, X),
            dense(STEPS, 7, X),
            dense(2, X),
            dense(STEPS - 1, X),
            dense(STEPS, 2, X),
            dense(X),
            dense(X + 1),
            tall(X),
            dense(X),
            pltpu.VMEM((3, ROWS, Z), F32),
            dense(rounds, 2),
            dense(rounds, 2),
            pltpu.VMEM((rounds, 2, face_rows, Z), F32),
            pltpu.VMEM((rounds, 2, face_rows, Z), F32),
            pltpu.VMEM((3, 8, Z), F32),
            pltpu.VMEM((sizes[0], 8, Z), F32),
            pltpu.VMEM((sizes[1], 8, Z), F32),
            pltpu.VMEM((sizes[2], 8, Z), F32),
            pltpu.SemaphoreType.DMA((copies,)),
            pltpu.SemaphoreType.DMA((copies,)),
            pltpu.SemaphoreType.DMA((lines,)),
            pltpu.SemaphoreType.DMA((lines,)),
            pltpu.SemaphoreType.DMA((11,)),
        ],
        compiler_params=pltpu.CompilerParams(
            collective_id=0, has_side_effects=True, vmem_limit_bytes=56 * 1024 * 1024
        ),
    )(*args[:7], *stims)
    return hess, curv.reshape(())


def solution(mesh):
    sizes = tuple(mesh.shape[a] for a in AXES)
    split = P(*AXES)
    return jax.shard_map(
        partial(shards, sizes),
        mesh=mesh,
        in_specs=(split,) * 7 + (P(),) * 4,
        out_specs=(split, P()),
        check_vma=False,
    )
```
